128 devices in a mesh: dp: 16 (over z, x_lo, core), factor: 8 (over x_hi, y).
Axes of the slice: x: 4 (x_hi: 2, x_lo: 2; x = x_hi * 2 + x_lo), y: 4, z: 4, core: 2. Of those that a mesh axis runs over, the one named last changes fastest.
Arguments:
- activations: bfloat16 [8192, 3072], P('dp'), may hold values from -6 to 6
- cotangents: bfloat16 [8192, 12288], P('dp', 'factor'), may hold values from -6 to 6
- basis_in: bfloat16 [1536, 2, 1536], P('dp', None, 'factor'), may hold values from -0.15625 to 0.15625
- basis_out: bfloat16 [12288, 1536], P('factor'), may hold values from -0.15625 to 0.15625
- factor_in: float32 [1536, 2, 1536], P('dp', None, 'factor'), may hold values from -0.15625 to 0.15625
- factor_out: float32 [1536, 12288], P('dp', 'factor'), may hold values from -0.15625 to 0.15625
- scale_in: float32 [2, 1536], replicated, may hold values from 0.02 to 0.3
- scale_out: float32 [12288], P('factor'), may hold values from 0.02 to 0.3
- overflow: int32 [8192], P('dp'), may hold values from 0 to 1, as said below
Outputs:
- precond: bfloat16 [1536, 2, 12288], P('dp', None, 'factor')
- new_factor_in: float32 [1536, 2, 1536], P('dp', None, 'factor')
- new_factor_out: float32 [1536, 12288], P('dp', 'factor')
The draws below stay inside these ranges and needn't reach their ends.
Inputs may be any that keep to these rules, and one draw needn't show every extreme that they name: `overflow`: rows of odd index are never marked; so at least half of the rows are healthy.
All inputs are finite; a program needn't handle non-finite values.
Results may differ from the reference program's by a relative error of at most 0.017.
Values may be sent and summed in bfloat16 or wider, within the bound.
No kernel may reach another device: no remote copies, remote signals or barrier semaphores. Data moves between devices by JAX's collectives and lax.ppermute only.
A program may use at most 128 MiB of HBM per device.

```python
import math
import jax
import jax.numpy as jnp
from jax import lax

BLK = 1536
NA = 2
TOK_DEV = 512
DW = 3072
FFW = 12288
TOKENS = 8192
N_DP = 16
N_FACTOR = 8


def draw_overflow(key, part):
    key = jax.random.fold_in(key, 7)
    position = jnp.arange(TOKENS, dtype=jnp.int32)
    levels = jax.random.randint(key, (TOKENS,), 0, 1000)
    limits = 1000 * position // TOKENS
    marked = (position % 2 == 0) & (levels < limits)
    return marked.astype(jnp.int32)


def steps_of(own_key, extent, split, smallest, high):
    def one(dim, blocks):
        heights = jax.random.uniform(jax.random.fold_in(jax.random.fold_in(own_key, 6), dim), (blocks,), jnp.float32, smallest / len(split), high / len(split))
        return jnp.repeat(jnp.exp(heights), extent[dim] // blocks).reshape((-1,) + (1,) * (len(extent) - dim - 1))

    loudness = one(*split[0])
    for cut in split[1:]:
        loudness = loudness * one(*cut)
    return loudness


def scatter_about(key, shape, deviation, limit, shards=(), kind=jnp.bfloat16):
    level = steps_of(key, shape, shards, -0.22, 0.18) if shards else 1.0
    drawn = jax.random.normal(key, shape, jnp.float32) * deviation * level
    return jnp.minimum(jnp.maximum(drawn, -limit), limit).astype(kind)


def setup_inputs(seed: int = 0) -> dict:
    seeds = jax.random.split(jax.random.key(seed), 10)
    activations = scatter_about(seeds[0], (TOKENS, DW), 1.0, 6.0, ((0, 16),))
    cotangents = scatter_about(seeds[1], (TOKENS, FFW), 1.0, 6.0, ((0, 16), (1, 8)))
    basis_in = scatter_about(seeds[2], (BLK, NA, BLK), BLK ** -0.5, 0.15625, ((0, 16), (2, 8)))
    basis_out = scatter_about(seeds[3], (FFW, BLK), BLK ** -0.5, 0.15625, ((0, 8),))
    factor_in = scatter_about(seeds[4], (BLK, NA, BLK), 0.01, 0.15625, ((0, 16), (2, 8)), jnp.float32)
    factor_out = scatter_about(seeds[5], (BLK, FFW), 0.01, 0.15625, ((0, 16), (1, 8)), jnp.float32)
    scale_in = jnp.clip(jnp.exp(jax.random.uniform(seeds[6], (NA, BLK), jnp.float32, math.log(0.02), math.log(0.3))), 0.02, 0.3)
    scale_out = jnp.clip(jnp.exp(math.log(0.3) - 2.7080503 * jax.random.uniform(seeds[7], (FFW,), jnp.float32) ** steps_of(seeds[7], (FFW,), ((0, 8),), -0.2, 0.2)), 0.02, 0.3)
    overflow = draw_overflow(jax.random.fold_in(seeds[9], 71), 0)
    return {"activations": activations, "cotangents": cotangents, "basis_in": basis_in, "basis_out": basis_out, "factor_in": factor_in, "factor_out": factor_out, "scale_in": scale_in, "scale_out": scale_out, "overflow": overflow}


decay_rate = 0.9
damping = 0.001


def rounded(value):
    return lax.optimization_barrier(value.astype(jnp.bfloat16)).astype(jnp.float32)


def reference(activations, cotangents, basis_in, basis_out, factor_in, factor_out, scale_in, scale_out, overflow):
    healthy = (overflow == 0)[:, None]
    input_masked_rows = jnp.where(healthy, activations, jnp.zeros_like(activations)).reshape(TOKENS, NA, BLK)
    masked_out = jnp.where(healthy, cotangents, jnp.zeros_like(cotangents)).reshape(TOKENS, N_FACTOR, BLK)
    healthy_rows = jnp.float32(TOKENS) - jnp.sum(overflow.astype(jnp.float32))
    out_blocks = basis_out.reshape(N_FACTOR, BLK, BLK).astype(jnp.float32)
    eigen_in = jnp.einsum("tar,rak->tak", input_masked_rows.astype(jnp.float32), basis_in.astype(jnp.float32)).astype(jnp.bfloat16)
    output_eigenvalues = jnp.einsum("tjm,jmg->tjg", masked_out.astype(jnp.float32), out_blocks).astype(jnp.bfloat16)
    in_total = jnp.sum(jnp.square(eigen_in.astype(jnp.float32)), axis=0)
    out_total = jnp.sum(jnp.square(output_eigenvalues.astype(jnp.float32)), axis=0)
    grouped = (eigen_in.reshape(N_DP, TOK_DEV, NA, BLK), output_eigenvalues.reshape(N_DP, TOK_DEV, N_FACTOR, BLK),
               input_masked_rows.reshape(N_DP, TOK_DEV, NA, BLK), masked_out.reshape(N_DP, TOK_DEV, N_FACTOR, BLK))

    def add_group(running, portion):
        rot_in, rot_out, unmasked_input, raw_out = portion
        grad_part = jnp.einsum("tak,tjg->kajg", rot_in.astype(jnp.float32), rot_out.astype(jnp.float32))
        input_slice = jnp.einsum("eku,eks->uks", unmasked_input.astype(jnp.float32), unmasked_input.astype(jnp.float32))
        out_part = jnp.einsum("tjr,tjc->rjc", raw_out.astype(jnp.float32), raw_out.astype(jnp.float32))
        return (running[0] + rounded(grad_part), running[1] + rounded(input_slice), running[2] + rounded(out_part)), None

    start_sums = (jnp.zeros((BLK, NA, N_FACTOR, BLK), jnp.float32), jnp.zeros((BLK, NA, BLK), jnp.float32),
                  jnp.zeros((BLK, N_FACTOR, BLK), jnp.float32))
    sums, _ = lax.scan(add_group, start_sums, grouped)
    grad_sum, cov_in_sum, cov_out_sum = sums
    blend_weight = 1.0 - decay_rate
    new_factor_in = decay_rate * factor_in + blend_weight * cov_in_sum / healthy_rows
    new_factor_out = decay_rate * factor_out + blend_weight * cov_out_sum.reshape(BLK, FFW) / healthy_rows
    input_eigenvalues = decay_rate * scale_in + blend_weight * in_total / healthy_rows
    lam_out = decay_rate * scale_out.reshape(N_FACTOR, BLK) + blend_weight * out_total / healthy_rows
    denominator = input_eigenvalues.T[:, :, None, None] * lam_out[None, None, :, :] + damping
    scaled = ((grad_sum / healthy_rows) / denominator).astype(jnp.bfloat16)
    turned = jnp.einsum("kajg,jmg->kajm", scaled.astype(jnp.float32), out_blocks).astype(jnp.bfloat16)
    precond = jnp.einsum("rak,kajm->rajm", basis_in.astype(jnp.float32), turned.astype(jnp.float32))
    precond = precond.reshape(BLK, NA, FFW).astype(jnp.bfloat16)
    return precond, new_factor_in, new_factor_out
```

```python
import jax
import jax.numpy as jnp
from jax import lax
from jax.experimental import pallas as pl
from jax.experimental.pallas import tpu as pltpu
from jax.sharding import PartitionSpec as P

decay_rate = 0.9
damping = 0.001
blend_weight = 1.0 - decay_rate

f32 = jnp.float32
bf16 = jnp.bfloat16

CORE = [(i, i ^ 1) for i in range(16)]
XLO = [(i, i ^ 2) for i in range(16)]
XHI = [(j, j ^ 4) for j in range(8)]
SAME_XHI = [[0, 1, 2, 3], [4, 5, 6, 7]]
PARAMS = pltpu.CompilerParams(vmem_limit_bytes=56 * 2**20)


def to_z(s):
    return [(i, ((i >> 2) + s) % 4 * 4 + (i & 3)) for i in range(16)]


def swap_z(bits):
    return [(i, i ^ (bits * 4)) for i in range(16)]


def swap_y(bits):
    return [(j, j ^ bits) for j in range(8)]


UP, DOWN = to_z(1), to_z(3)


def dot(a, b, contract=((1,), (0,)), **kwargs):
    return lax.dot_general(a, b, (contract, ((), ())), preferred_element_type=f32, **kwargs)


def added(*parts):
    total = parts[0].astype(f32)
    for part in parts[1:]:
        total = total + part.astype(f32)
    return total


def after(value, *others):
    return lax.optimization_barrier((value, *others))[0]


def send_z(up, down):
    return lax.ppermute(up, "dp", UP), lax.ppermute(down, "dp", DOWN)


def forward_z(got_up, got_down, first_1, second_3):
    return added(first_1, got_up[0]).astype(bf16), added(second_3, got_down[0]).astype(bf16)


def shape_of(*dims, dtype=bf16):
    return jax.ShapeDtypeStruct(dims, dtype)


def whole(shape):
    return pl.BlockSpec(shape, lambda *_: (0,) * len(shape))


def placed(kernel, place, grid, in_specs, out_shapes, operands, out_specs=None, scratch=()):
    return pl.pallas_call(
        kernel,
        out_shape=out_shapes,
        grid_spec=pltpu.PrefetchScalarGridSpec(
            num_scalar_prefetch=1,
            grid=grid,
            in_specs=in_specs,
            out_specs=out_specs or [whole(s.shape) for s in out_shapes],
            scratch_shapes=list(scratch),
        ),
        compiler_params=PARAMS,
        name=kernel.__name__,
    )(place, *operands)


def healthy(marks):
    return (marks[...] == 0).astype(f32)


def rotate_kernel(place, cot, marks, basis, *refs):
    refs[-1][...] = jnp.swapaxes(dot(cot[...], basis[...]).astype(bf16), 0, 1) * healthy(marks).astype(bf16)


def grad_kernel(place, eigen_0, eigen_1, act_0, act_1, give, keep, up, down, first_1, second_3, own, total):
    chunk, cut = give.shape[1], give.shape[2]
    total[...] = dot(eigen_0[...], act_0[...]) + dot(eigen_1[...], act_1[...])
    outs = ((own, 0, own, 1), (first_1, None, up, 1), (up, 0, down, 0), (down, 1, second_3, None))
    for s in range(4):
        base = (place[0] + s) % 4 * 2 * chunk
        mine = pl.ds(pl.multiple_of(base + place[1] * chunk, 16), chunk)
        other = pl.ds(pl.multiple_of(base + (1 - place[1]) * chunk, 16), chunk)
        give[s] = total[other, :cut].astype(bf16)
        keep[s] = total[mine, :cut].astype(bf16)
        for half in range(2):
            out, at = outs[s][2 * half : 2 * half + 2]
            value = total[pl.ds(pl.multiple_of(base + half * chunk, 16), chunk), cut:].astype(bf16)
            if at is None:
                out[...] = value
            else:
                out[at] = value


def second_kernel(keep, got_a, got_up, got_down, first_1, second_3, up, down, a_first_1, a_second_3, own_a):
    part = own_a.shape[1]
    rest = first_1.shape[1]
    up[:, :rest] = added(first_1[...], got_up[0]).astype(bf16)
    down[:, :rest] = added(second_3[...], got_down[0]).astype(bf16)

    def a_sum(s, half):
        rows = slice(half * part, (half + 1) * part)
        return added(keep[s, rows], got_a[s, rows]).astype(bf16)

    up[:part, rest:] = a_sum(2, 0)
    up[part:, rest:] = a_sum(1, 1)
    down[:part, rest:] = a_sum(2, 1)
    down[part:, rest:] = a_sum(3, 0)
    a_first_1[...] = a_sum(1, 0)
    a_second_3[...] = a_sum(3, 1)
    own_a[0] = a_sum(0, 0)
    own_a[1] = a_sum(0, 1)


def third_kernel(
    place, got_up, got_down, up, down, own_b, a_first_1, a_second_3, own_a, a_up, a_down, give, keep_b, keep_a
):
    part = own_a.shape[1]
    rest = own_b.shape[2]
    a_up[...] = added(a_first_1[...], up[:part, rest:]).astype(bf16)
    a_down[...] = added(a_second_3[...], down[:part, rest:]).astype(bf16)
    first = added(own_b[0], got_down[0], up[:, :rest])
    second = added(own_b[1], got_up[0], down[:, :rest])
    left = place[1] == 0
    give[...] = jnp.where(left, second, first).astype(bf16)
    keep_b[...] = jnp.where(left, first, second)
    keep_a[0] = added(own_a[0], down[part:, rest:])
    keep_a[1] = added(own_a[1], up[part:, rest:])


def cov_kernel(
    place, cot_0, cot_1, marks_0, marks_1, rows_0, rows_1, act_0, act_1, cols_0, cols_1, up, down, rest, turned, mine
):
    places = (((rest, 0), (rest, 2), (up, 0), (down, 1)), ((rest, 1), (up, 1), (down, 0), (rest, 3)))
    tokens = cot_0.shape[0]
    rows = turned.shape[0] // 4
    mask_0, mask_1 = healthy(marks_0).astype(bf16), healthy(marks_1).astype(bf16)
    turned[:, :tokens] = jnp.swapaxes(rows_0[...], 0, 1) * mask_0
    turned[:, tokens:] = jnp.swapaxes(rows_1[...], 0, 1) * mask_1
    for x in range(2):
        mine[x * rows : (x + 1) * rows] = turned[pl.ds(pl.multiple_of((2 * x + place[2]) * rows, 16), rows), :]
    cov_out = dot(mine[:, :tokens], cot_0[...]) + dot(mine[:, tokens:], cot_1[...])
    odd = place[3] % 2
    own = [jnp.where(odd == 0, c[:, : 2 * rows].astype(f32), c[:, 2 * rows :].astype(f32)).astype(bf16) for c in (cols_0, cols_1)]
    cov_in = dot(jnp.swapaxes(act_0[...], 0, 1) * mask_0, own[0])
    cov_in += dot(jnp.swapaxes(act_1[...], 0, 1) * mask_1, own[1])
    for x in range(2):
        low = 2 * x * rows
        pair = jnp.concatenate([cov_in[low : low + rows], cov_in[low + rows : low + 2 * rows]], 1)
        value = jnp.concatenate([cov_out[x * rows : (x + 1) * rows], pair], 1).astype(bf16)
        for s, (out, at) in enumerate(places[x]):

            @pl.when(pl.program_id(0) == s)
            def _():
                out[at] = value


def squares_kernel(place, act_0, act_1, marks_0, marks_1, basis, eigen_0, eigen_1, out_in, out_out):
    total = 0.0
    for act, marks in ((act_0, marks_0), (act_1, marks_1)):
        tokens, columns = act.shape[0], basis.shape[1]
        lanes = min(128, columns)
        square = jnp.square(dot(act[...], basis[...]).astype(bf16).astype(f32))
        mask = jnp.swapaxes(jnp.broadcast_to(healthy(marks), (lanes, tokens)), 0, 1)
        total += jnp.sum(square * jnp.concatenate([mask] * (columns // lanes), 1), axis=0, keepdims=True)
    out_in[...] = total
    width, tokens = eigen_0.shape
    lanes = min(128, tokens)
    for at in range(0, width, width // 4):
        rows = slice(at, at + width // 4)
        square = jnp.square(eigen_0[rows].astype(f32)) + jnp.square(eigen_1[rows].astype(f32))
        square = sum(square[:, i : i + lanes] for i in range(0, tokens, lanes))
        out_out[:, rows] = jnp.sum(jnp.swapaxes(square, 0, 1), axis=0, keepdims=True)


def rows_kernel(place, own, got, out):
    for s in range(4):
        out[(place[0] + s) % 4, place[1]] = own[s]
        out[(place[0] + s) % 4, 1 - place[1]] = got[s]


def turn_kernel(keep_a, via_up, via_down, keep_b, got_b, basis, lam_out, lam_in, damp, out, grad, total):
    y = pl.program_id(0)
    cut = keep_a.shape[2]
    part = keep_a.shape[1]

    @pl.when(y == 0)
    def _():
        grad[:part, :cut] = added(keep_a[0], via_up[...]).astype(bf16)
        grad[part:, :cut] = added(keep_a[1], via_down[...]).astype(bf16)
        grad[:, cut:] = added(keep_b[...], got_b[...]).astype(bf16)
        total[...] = jnp.zeros(total.shape, f32)

    rotated = dot(grad[...], basis[0])
    scaled = (rotated / (lam_out[...] * lam_in[0] + damp[...])).astype(bf16)
    total[...] += dot(basis[0], scaled, ((1,), (1,)))

    @pl.when(y == 3)
    def _():
        out[...] = total[...].astype(bf16)


def last_kernel(spread, basis_out, out):
    chunk = spread.shape[2]
    rows = spread.shape[1]
    total = None
    for z in range(4):
        lhs = jnp.concatenate(
            [jnp.concatenate([spread[4 * z + a], spread[4 * z + 2 + a]], 1) for a in range(2)], 0
        )
        part = dot(lhs, basis_out[:, 2 * z * chunk : 2 * (z + 1) * chunk], ((1,), (1,)))
        total = part if total is None else total + part
    out[0] = total[:rows].astype(bf16)
    out[1] = total[rows:].astype(bf16)


def per_device(
    activations,
    cotangents,
    basis_in,
    basis_out,
    factor_in,
    factor_out,
    scale_in,
    scale_out,
    overflow,
):
    tokens = activations.shape[0]
    width = scale_in.shape[1]
    rows = factor_in.shape[0]
    cols = factor_in.shape[2]
    chunk = width // 8
    wide = width // 4
    cut = width // 3
    dp = lax.axis_index("dp")
    fac = lax.axis_index("factor")
    core, x, z = dp % 2, (dp // 2) % 2, dp // 4
    place = jnp.stack([z, x, core, fac]).astype(jnp.int32)

    basis_keep = lax.dynamic_index_in_dim(basis_in, core, 1, keepdims=False)
    basis_give = lax.dynamic_index_in_dim(basis_in, 1 - core, 1, keepdims=False)
    basis_got = lax.ppermute(basis_give, "dp", CORE)
    marks = overflow.reshape(1, tokens)
    marks_got = lax.ppermute(marks, "dp", CORE)
    cot_got = lax.ppermute(cotangents, "dp", CORE)
    act_give = lax.dynamic_slice_in_dim(activations, (1 - core) * width, width, 1)
    act_got = lax.ppermute(act_give, "dp", CORE)

    def rotate(place, at, before):
        return pl.pallas_call(
            rotate_kernel,
            out_shape=shape_of(width, tokens),
            grid_spec=pltpu.PrefetchScalarGridSpec(
                num_scalar_prefetch=1,
                grid=(2,),
                in_specs=[
                    whole((tokens, width)),
                    whole((1, tokens)),
                    pl.BlockSpec((width, wide), lambda i, p: (0, at + i)),
                ]
                + [pl.BlockSpec(memory_space=pl.ANY)] * len(before),
                out_specs=pl.BlockSpec((wide, tokens), lambda i, p: (at + i, 0)),
            ),
            input_output_aliases={4: 0} if before else {},
            compiler_params=PARAMS,
            name="rotate_kernel",
        )(place, cotangents, marks, basis_out, *before)

    eigen_half = rotate(after(place, act_give, basis_give), 0, ())
    basis_mine = after(basis_keep, eigen_half)
    basis_chip = jnp.where(
        core == 0,
        jnp.concatenate([basis_mine, basis_got], 0),
        jnp.concatenate([basis_got, basis_mine], 0),
    )
    basis_x_hi = lax.ppermute(basis_chip, "factor", XHI)
    eigen = rotate(after(place, basis_chip, marks_got), 2, (eigen_half,))
    eigen_got = lax.ppermute(after(eigen, basis_x_hi), "dp", CORE)
    basis_pair = jnp.concatenate([after(basis_chip, eigen), basis_x_hi], 1)
    basis_z = [lax.ppermute(basis_pair, "dp", to_z(4 - s)) for s in (1, 2, 3)]

    def own_block(n, at):
        return pl.BlockSpec((tokens, n), lambda i, p: (0, at(i, p)))

    columns = width + 2 * cols
    cov_up, cov_down, cov_rest = placed(
        cov_kernel,
        after(place, basis_pair),
        (4,),
        [whole((tokens, width))] * 2
        + [whole((1, tokens))] * 2
        + [own_block(wide, lambda i, p: (p[0] + i) % 4)] * 2
        + [own_block(wide, lambda i, p: p[2] * 4 + (p[0] + i) % 4), own_block(wide, lambda i, p: (p[0] + i) % 4)]
        + [own_block(wide, lambda i, p: p[2] * 4 + p[3] // 2), own_block(wide, lambda i, p: p[3] // 2)],
        [shape_of(n, rows, columns) for n in (2, 2, 4)],
        (cotangents, cot_got, marks, marks_got, cotangents, cot_got, activations, act_got, activations, act_got),
        scratch=[pltpu.VMEM((wide, 2 * tokens), bf16), pltpu.VMEM((wide // 2, 2 * tokens), bf16)],
    )
    cov_got_up, cov_got_down = send_z(cov_up, cov_down)

    basis_four = jnp.stack([after(basis_pair, cov_up), *basis_z])
    basis_x_lo = lax.ppermute(basis_four, "dp", XLO)

    single = shape_of(chunk, width - cut)
    pair = shape_of(2, chunk, width - cut)
    four = shape_of(4, chunk, cut)
    give, keep, up, down, first_1, second_3, own_b = placed(
        grad_kernel,
        after(place, basis_four),
        (1,),
        [whole((width, tokens))] * 2
        + [pl.BlockSpec((tokens, width), lambda i, p: (0, p[2])), whole((tokens, width))],
        [four, four, pair, pair, single, single, pair],
        (eigen, eigen_got, activations, act_got),
        scratch=[pltpu.VMEM((width, width), f32)],
    )
    (basis_rows,) = placed(
        rows_kernel,
        after(place, own_b, cov_got_up, cov_got_down),
        (1,),
        [whole(basis_four.shape)] * 2,
        [shape_of(4, 2, 2 * rows, 2 * cols)],
        (basis_four, basis_x_lo),
    )
    basis_rows = basis_rows.reshape(width, 2 * cols)
    basis_all = lax.all_gather(basis_rows, "factor", axis=0, axis_index_groups=SAME_XHI)
    squares_in, squares_out = placed(
        squares_kernel,
        place,
        (1,),
        [pl.BlockSpec((tokens, width), lambda i, p: (0, p[2])), whole((tokens, width))]
        + [whole((1, tokens))] * 2
        + [whole((width, 2 * cols))]
        + [whole((width, tokens))] * 2,
        [shape_of(1, 2 * cols, dtype=f32), shape_of(1, width, dtype=f32)],
        (activations, act_got, marks, marks_got, basis_rows, eigen, eigen_got),
    )
    by_y = jnp.concatenate([squares_in, lax.ppermute(squares_in, "factor", swap_y(1))], 0)
    by_y = jnp.concatenate([by_y, lax.ppermute(by_y, "factor", swap_y(2))], 0)
    count = jnp.sum((marks + marks_got).astype(f32))
    small = jnp.concatenate([squares_out[0], jnp.full((128,), count), by_y.reshape(width)])
    give, up, down = lax.optimization_barrier((give, up, down, basis_x_lo))[:3]
    got_a = lax.ppermute(give, "dp", XLO)
    got_up, got_down = send_z(up, down)
    part = chunk // 2
    second_up, second_down, a_first_1, a_second_3, own_a = pl.pallas_call(
        second_kernel,
        out_shape=(
            shape_of(chunk, width),
            shape_of(chunk, width),
            shape_of(part, cut),
            shape_of(part, cut),
            shape_of(2, part, cut),
        ),
        compiler_params=PARAMS,
        name="second_kernel",
    )(after(keep, by_y, cov_got_up, cov_got_down), got_a, got_up, got_down, first_1, second_3)
    second_got_up, second_got_down = send_z(second_up, second_down)

    small = after(small, second_up)
    small = small + lax.ppermute(small, "dp", XLO)
    small = small + lax.ppermute(small, "dp", swap_z(1))
    y = fac % 4
    near = pl.BlockSpec((1, chunk, width - cut), lambda i, p: (1, 0, 0))
    third_in = (second_got_up, second_got_down, own_b, a_first_1, a_second_3, own_a)
    third_up, third_down, b_give, b_keep, a_keep = placed(
        third_kernel,
        after(place, small),
        (1,),
        [near, near] + [whole(t.shape) for t in third_in],
        [
            shape_of(part, cut),
            shape_of(part, cut),
            shape_of(chunk, width - cut),
            shape_of(chunk, width - cut, dtype=f32),
            shape_of(2, part, cut, dtype=f32),
        ],
        (got_up, got_down, *third_in),
    )
    b_got = lax.ppermute(b_give, "dp", XLO)
    a_via_up, a_via_down = send_z(third_up, third_down)
    small = after(small, b_give)
    small = small + lax.ppermute(small, "dp", swap_z(3))

    healthy_rows = f32(tokens * lax.axis_size("dp")) - small[width]
    out_total = lax.dynamic_slice_in_dim(small, (z * 2 + x) * chunk, chunk, 0)
    in_total = small[width + 128 :].reshape(2, 2, 2 * cols)
    in_total = jnp.where(y % 2 == 0, in_total, in_total[:, ::-1])
    in_total = jnp.where(y < 2, in_total, in_total[::-1]).reshape(4, 2 * cols)

    cov_next = forward_z(cov_got_up, cov_got_down, cov_rest[2], cov_rest[3])
    cov_next = lax.optimization_barrier((*cov_next, b_give))[:2]
    cov_via_up, cov_via_down = send_z(*cov_next)

    cov_first = added(cov_rest[0], cov_got_down[1], cov_via_up)
    cov_second = added(cov_rest[1], cov_got_up[1], cov_via_down)
    cov_give = jnp.where(x == 0, cov_second, cov_first).astype(bf16)
    cov_keep = jnp.where(x == 0, cov_first, cov_second)
    cov_give = after(cov_give, basis_all)
    cov_sum = added(cov_keep, lax.ppermute(cov_give, "dp", XLO))
    sum_out = cov_sum[:, :width]
    sum_in = cov_sum[:, width:].reshape(rows, 2, cols)
    in_keep = lax.dynamic_index_in_dim(sum_in, core, 1, keepdims=False)
    in_give = lax.dynamic_index_in_dim(sum_in, 1 - core, 1, keepdims=False).astype(bf16)
    in_got = lax.ppermute(in_give, "dp", CORE).astype(f32)

    scale_own = lax.dynamic_index_in_dim(scale_in, core, 0, keepdims=False).reshape(2, 4, cols)
    scale_own = jnp.where(fac // 4 == 0, scale_own, scale_own[::-1])
    scale_own = jnp.concatenate([scale_own[0], scale_own[1]], 1)
    lam_in = decay_rate * scale_own + blend_weight * in_total / healthy_rows
    scale_chip = lax.dynamic_slice_in_dim(scale_out, (z * 2 + x) * chunk, chunk, 0)
    lam_out = decay_rate * scale_chip + blend_weight * out_total / healthy_rows
    lam_out = (lam_out * healthy_rows)[:, None]
    damp = jnp.full((1, 2 * cols), damping * healthy_rows)

    turn_in = (a_keep, a_via_up, a_via_down, b_keep, b_got)
    turned = pl.pallas_call(
        turn_kernel,
        out_shape=shape_of(width, chunk),
        grid=(4,),
        in_specs=[whole(t.shape) for t in turn_in]
        + [pl.BlockSpec((1, width, 2 * cols), lambda i: (i, 0, 0)), whole((chunk, 1))]
        + [pl.BlockSpec((1, 1, 2 * cols), lambda i: (i, 0, 0)), whole((1, 2 * cols))],
        out_specs=whole((width, chunk)),
        scratch_shapes=[pltpu.VMEM((chunk, width), bf16), pltpu.VMEM((width, chunk), f32)],
        compiler_params=PARAMS,
        name="turn_kernel",
    )(*turn_in, basis_all, lam_out, lam_in[:, None], damp)
    spread = lax.all_to_all(turned.reshape(16, rows, chunk), "dp", split_axis=0, concat_axis=0)
    result = pl.pallas_call(
        last_kernel, out_shape=shape_of(2, rows, width), compiler_params=PARAMS, name="last_kernel"
    )(spread, basis_out)

    sum_in = jnp.where(core == 0, jnp.stack([in_keep, in_got], 1), jnp.stack([in_got, in_keep], 1))
    new_factor_in = decay_rate * factor_in + blend_weight * sum_in / healthy_rows
    new_factor_out = decay_rate * factor_out + blend_weight * sum_out / healthy_rows
    return (jnp.swapaxes(result, 0, 1), new_factor_in, new_factor_out)


def solution(mesh):
    in_specs = (
        P("dp", None),
        P("dp", "factor"),
        P("dp", None, "factor"),
        P("factor", None),
        P("dp", None, "factor"),
        P("dp", "factor"),
        P(),
        P("factor"),
        P("dp"),
    )
    out_specs = (P("dp", None, "factor"), P("dp", None, "factor"), P("dp", "factor"))
    return jax.shard_map(
        per_device, mesh=mesh, in_specs=in_specs, out_specs=out_specs, check_vma=False
    )
```

```python
import functools

import jax
import jax.numpy as jnp
from jax import lax
from jax.experimental import pallas as pl
from jax.experimental.pallas import tpu as pltpu
from jax.sharding import PartitionSpec as P

decay_rate = 0.9
damping = 0.001
blend_weight = 1.0 - decay_rate

f32 = jnp.float32
bf16 = jnp.bfloat16

CORE = [(i, i ^ 1) for i in range(16)]
XLO = [(i, i ^ 2) for i in range(16)]
XHI = [(j, j ^ 4) for j in range(8)]
SAME_XHI = [[0, 1, 2, 3], [4, 5, 6, 7]]
PARAMS = pltpu.CompilerParams(vmem_limit_bytes=56 * 2**20)


def to_z(s):
    return [(i, ((i >> 2) + s) % 4 * 4 + (i & 3)) for i in range(16)]


def swap_z(bits):
    return [(i, i ^ (bits * 4)) for i in range(16)]


def swap_y(bits):
    return [(j, j ^ bits) for j in range(8)]


UP, DOWN = to_z(1), to_z(3)


def dot(a, b, contract=((1,), (0,)), **kwargs):
    return lax.dot_general(a, b, (contract, ((), ())), preferred_element_type=f32, **kwargs)


def added(*parts):
    total = parts[0].astype(f32)
    for part in parts[1:]:
        total = total + part.astype(f32)
    return total


def after(value, *others):
    return lax.optimization_barrier((value, *others))[0]


def send_z(up, down):
    return lax.ppermute(up, "dp", UP), lax.ppermute(down, "dp", DOWN)


def forward_z(got_up, got_down, first_1, second_3):
    return added(first_1, got_up[0]).astype(bf16), added(second_3, got_down[0]).astype(bf16)


def shape_of(*dims, dtype=bf16):
    return jax.ShapeDtypeStruct(dims, dtype)


def whole(shape):
    return pl.BlockSpec(shape, lambda *_: (0,) * len(shape))


def placed(kernel, place, grid, in_specs, out_shapes, operands, out_specs=None, scratch=(), name=None):
    return pl.pallas_call(
        kernel,
        out_shape=out_shapes,
        grid_spec=pltpu.PrefetchScalarGridSpec(
            num_scalar_prefetch=1,
            grid=grid,
            in_specs=in_specs,
            out_specs=out_specs or [whole(s.shape) for s in out_shapes],
            scratch_shapes=list(scratch),
        ),
        compiler_params=PARAMS,
        name=name or kernel.__name__,
    )(place, *operands)


def healthy(marks):
    return (marks[...] == 0).astype(f32)


def rotate_kernel(place, cot, marks, basis, *refs):
    refs[-1][...] = jnp.swapaxes(dot(cot[...], basis[...]).astype(bf16), 0, 1) * healthy(marks).astype(bf16)


def grad_kernel(place, eigen_0, eigen_1, act_0, act_1, give, keep, up, down, first_1, second_3, own, total):
    chunk, cut = give.shape[1], give.shape[2]
    total[...] = dot(eigen_0[...], act_0[...]) + dot(eigen_1[...], act_1[...])
    outs = ((own, 0, own, 1), (first_1, None, up, 1), (up, 0, down, 0), (down, 1, second_3, None))
    for s in range(4):
        base = (place[0] + s) % 4 * 2 * chunk
        mine = pl.ds(pl.multiple_of(base + place[1] * chunk, 16), chunk)
        other = pl.ds(pl.multiple_of(base + (1 - place[1]) * chunk, 16), chunk)
        give[s] = total[other, :cut].astype(bf16)
        keep[s] = total[mine, :cut].astype(bf16)
        for half in range(2):
            out, at = outs[s][2 * half : 2 * half + 2]
            value = total[pl.ds(pl.multiple_of(base + half * chunk, 16), chunk), cut:].astype(bf16)
            if at is None:
                out[...] = value
            else:
                out[at] = value


def second_kernel(keep, got_a, got_up, got_down, first_1, second_3, up, down, a_first_1, a_second_3, own_a):
    part = own_a.shape[1]
    rest = first_1.shape[1]
    up[:, :rest] = added(first_1[...], got_up[0]).astype(bf16)
    down[:, :rest] = added(second_3[...], got_down[0]).astype(bf16)

    def a_sum(s, half):
        rows = slice(half * part, (half + 1) * part)
        return added(keep[s, rows], got_a[s, rows]).astype(bf16)

    up[:part, rest:] = a_sum(2, 0)
    up[part:, rest:] = a_sum(1, 1)
    down[:part, rest:] = a_sum(2, 1)
    down[part:, rest:] = a_sum(3, 0)
    a_first_1[...] = a_sum(1, 0)
    a_second_3[...] = a_sum(3, 1)
    own_a[0] = a_sum(0, 0)
    own_a[1] = a_sum(0, 1)


def third_kernel(
    place, got_up, got_down, up, down, own_b, a_first_1, a_second_3, own_a, a_up, a_down, give, keep_b, keep_a
):
    part = own_a.shape[1]
    rest = own_b.shape[2]
    a_up[...] = added(a_first_1[...], up[:part, rest:]).astype(bf16)
    a_down[...] = added(a_second_3[...], down[:part, rest:]).astype(bf16)
    first = added(own_b[0], got_down[0], up[:, :rest])
    second = added(own_b[1], got_up[0], down[:, :rest])
    left = place[1] == 0
    give[...] = jnp.where(left, second, first).astype(bf16)
    keep_b[...] = jnp.where(left, first, second)
    keep_a[0] = added(own_a[0], down[part:, rest:])
    keep_a[1] = added(own_a[1], up[part:, rest:])


def cov_kernel(
    place, cot_0, cot_1, marks_0, marks_1, act_0, act_1, cols_0, cols_1, up, down, rest, turned, mine, cov_out, cov_in
):
    places = ((rest, 0, rest, 1), (rest, 2, up, 1), (up, 0, down, 0), (down, 1, rest, 3))
    tokens = cot_0.shape[0]
    rows = mine.shape[0] // 8
    mask_0, mask_1 = healthy(marks_0).astype(bf16), healthy(marks_1).astype(bf16)
    turned[:, :tokens] = jnp.swapaxes(cot_0[...], 0, 1) * mask_0
    turned[:, tokens:] = jnp.swapaxes(cot_1[...], 0, 1) * mask_1
    for s in range(4):
        for x in range(2):
            base = ((place[0] + s) % 4 * 4 + 2 * x + place[2]) * rows
            at = (2 * s + x) * rows
            mine[at : at + rows] = turned[pl.ds(pl.multiple_of(base, 16), rows), :]
    cov_out[...] = dot(mine[:, :tokens], cot_0[...]) + dot(mine[:, tokens:], cot_1[...])
    odd = place[3] % 2
    side = 0.0
    for cols, mask, act in ((cols_0, mask_0, act_0), (cols_1, mask_1, act_1)):
        own = jnp.where(odd == 0, cols[:, : 2 * rows].astype(f32), cols[:, 2 * rows :].astype(f32)).astype(bf16)
        side += dot(jnp.swapaxes(own, 0, 1) * mask, act[...])
    cov_in[...] = jnp.swapaxes(side, 0, 1)
    for s in range(4):
        for x in range(2):
            base = ((place[0] + s) % 4 * 4 + 2 * x) * rows
            pair = [cov_in[pl.ds(pl.multiple_of(base + k * rows, 16), rows), :] for k in range(2)]
            at = (2 * s + x) * rows
            out, index = places[s][2 * x : 2 * x + 2]
            out[index] = jnp.concatenate([cov_out[at : at + rows], *pair], 1).astype(bf16)


def squares_kernel(place, act_0, act_1, marks_0, marks_1, basis, eigen_0, eigen_1, out_in, out_out):
    total = 0.0
    for act, marks in ((act_0, marks_0), (act_1, marks_1)):
        tokens, columns = act.shape[0], basis.shape[1]
        lanes = min(128, columns)
        square = jnp.square(dot(act[...], basis[...]).astype(bf16).astype(f32))
        mask = jnp.swapaxes(jnp.broadcast_to(healthy(marks), (lanes, tokens)), 0, 1)
        total += jnp.sum(square * jnp.concatenate([mask] * (columns // lanes), 1), axis=0, keepdims=True)
    out_in[...] = total
    width, tokens = eigen_0.shape
    lanes = min(128, tokens)
    count = jnp.sum(2.0 - healthy(marks_0) - healthy(marks_1), axis=1, keepdims=True)
    out_out[4:5, :] = jnp.broadcast_to(count, (1, width // 4))
    for at in range(0, width, width // 4):
        rows = slice(at, at + width // 4)
        square = jnp.square(eigen_0[rows].astype(f32)) + jnp.square(eigen_1[rows].astype(f32))
        square = sum(square[:, i : i + lanes] for i in range(0, tokens, lanes))
        out_out[at // (width // 4) : at // (width // 4) + 1, :] = jnp.sum(jnp.swapaxes(square, 0, 1), axis=0, keepdims=True)


def rows_kernel(place, own, got, out):
    for s in range(4):
        out[(place[0] + s) % 4, place[1]] = own[s]
        out[(place[0] + s) % 4, 1 - place[1]] = got[s]


def turn_kernel(
    place, keep_a, via_up, via_down, keep_b, got_b, basis, small, scale_in, scale_out, out, grad, total, lam_out, rows_all
):
    y = pl.program_id(0)
    cut = keep_a.shape[2]
    part = keep_a.shape[1]
    chunk = 2 * part
    healthy_rows = rows_all - small[8:9, 0:1]

    @pl.when(y == 0)
    def _():
        grad[:part, :cut] = added(keep_a[0], via_up[...]).astype(bf16)
        grad[part:, :cut] = added(keep_a[1], via_down[...]).astype(bf16)
        grad[:, cut:] = added(keep_b[...], got_b[...]).astype(bf16)
        total[...] = jnp.zeros(total.shape, f32)
        lam = decay_rate * scale_out[pl.ds(place[0], 1), :] + blend_weight * small[pl.ds(place[0], 1), :] / healthy_rows
        lam = jnp.where(place[1] == 0, lam[:, :chunk], lam[:, chunk:]) * healthy_rows
        lam_out[...] = jnp.swapaxes(jnp.broadcast_to(lam, (lam_out.shape[1], chunk)), 0, 1)

    lam_in = decay_rate * scale_in[pl.ds(y, 1), :] + blend_weight * small[pl.ds(4 + y, 1), :] / healthy_rows
    rotated = dot(grad[...], basis[0])
    scaled = (rotated / (lam_out[:, :1] * lam_in + damping * healthy_rows)).astype(bf16)
    total[...] += dot(basis[0], scaled, ((1,), (1,)))

    @pl.when(y == 3)
    def _():
        out[...] = total[...].astype(bf16)


def last_kernel(spread, basis_out, out):
    chunk = spread.shape[2]
    rows = spread.shape[1]
    total = None
    for z in range(4):
        lhs = jnp.concatenate(
            [jnp.concatenate([spread[4 * z + a], spread[4 * z + 2 + a]], 1) for a in range(2)], 0
        )
        part = dot(lhs, basis_out[:, 2 * z * chunk : 2 * (z + 1) * chunk], ((1,), (1,)))
        total = part if total is None else total + part
    out[0] = total[:rows].astype(bf16)
    out[1] = total[rows:].astype(bf16)


def per_device(
    activations,
    cotangents,
    basis_in,
    basis_out,
    factor_in,
    factor_out,
    scale_in,
    scale_out,
    overflow,
):
    tokens = activations.shape[0]
    width = scale_in.shape[1]
    rows = factor_in.shape[0]
    cols = factor_in.shape[2]
    chunk = width // 8
    wide = width // 4
    cut = width // 3
    dp = lax.axis_index("dp")
    fac = lax.axis_index("factor")
    core, x, z = dp % 2, (dp // 2) % 2, dp // 4
    place = jnp.stack([z, x, core, fac]).astype(jnp.int32)

    basis_keep = lax.dynamic_index_in_dim(basis_in, core, 1, keepdims=False)
    basis_give = lax.dynamic_index_in_dim(basis_in, 1 - core, 1, keepdims=False)
    basis_got = lax.ppermute(basis_give, "dp", CORE)
    marks = overflow.reshape(1, tokens)
    marks_got = lax.ppermute(marks, "dp", CORE)
    cot_got = lax.ppermute(cotangents, "dp", CORE)
    act_give = lax.dynamic_slice_in_dim(activations, (1 - core) * width, width, 1)
    act_got = lax.ppermute(act_give, "dp", CORE)

    def rotate(place, at, before):
        return pl.pallas_call(
            rotate_kernel,
            out_shape=shape_of(width, tokens),
            grid_spec=pltpu.PrefetchScalarGridSpec(
                num_scalar_prefetch=1,
                grid=(2,),
                in_specs=[
                    whole((tokens, width)),
                    whole((1, tokens)),
                    pl.BlockSpec((width, wide), lambda i, p: (0, at + i)),
                ]
                + [pl.BlockSpec(memory_space=pl.ANY)] * len(before),
                out_specs=pl.BlockSpec((wide, tokens), lambda i, p: (at + i, 0)),
            ),
            input_output_aliases={4: 0} if before else {},
            compiler_params=PARAMS,
            name="rotate_kernel",
        )(place, cotangents, marks, basis_out, *before)

    eigen_half = rotate(after(place, act_give, basis_give), 0, ())
    basis_mine = after(basis_keep, eigen_half)
    basis_chip = jnp.where(
        core == 0,
        jnp.concatenate([basis_mine, basis_got], 0),
        jnp.concatenate([basis_got, basis_mine], 0),
    )
    basis_x_hi = lax.ppermute(basis_chip, "factor", XHI)
    eigen = rotate(after(place, basis_chip, marks_got), 2, (eigen_half,))
    eigen_got = lax.ppermute(after(eigen, basis_x_hi), "dp", CORE)
    basis_pair = jnp.concatenate([after(basis_chip, eigen), basis_x_hi], 1)
    basis_z = [lax.ppermute(basis_pair, "dp", to_z(4 - s)) for s in (1, 2, 3)]

    def own_block(n, at):
        return pl.BlockSpec((tokens, n), lambda i, p: (0, at(i, p)))

    columns = width + 2 * cols
    cov_up, cov_down, cov_rest = placed(
        cov_kernel,
        after(place, basis_pair),
        (1,),
        [whole((tokens, width))] * 2
        + [whole((1, tokens))] * 2
        + [own_block(width, lambda i, p: p[2]), whole((tokens, width))]
        + [own_block(wide, lambda i, p: p[2] * 4 + p[3] // 2), own_block(wide, lambda i, p: p[3] // 2)],
        [shape_of(n, rows, columns) for n in (2, 2, 4)],
        (cotangents, cot_got, marks, marks_got, activations, act_got, activations, act_got),
        scratch=[
            pltpu.VMEM((width, 2 * tokens), bf16),
            pltpu.VMEM((8 * rows, 2 * tokens), bf16),
            pltpu.VMEM((8 * rows, width), f32),
            pltpu.VMEM((width, cols), f32),
        ],
    )
    cov_got_up, cov_got_down = send_z(cov_up, cov_down)

    basis_four = jnp.stack([after(basis_pair, cov_up), *basis_z])
    basis_x_lo = lax.ppermute(basis_four, "dp", XLO)

    single = shape_of(chunk, width - cut)
    pair = shape_of(2, chunk, width - cut)
    four = shape_of(4, chunk, cut)
    give, keep, up, down, first_1, second_3, own_b = placed(
        grad_kernel,
        after(place, basis_four),
        (1,),
        [whole((width, tokens))] * 2
        + [pl.BlockSpec((tokens, width), lambda i, p: (0, p[2])), whole((tokens, width))],
        [four, four, pair, pair, single, single, pair],
        (eigen, eigen_got, activations, act_got),
        scratch=[pltpu.VMEM((width, width), f32)],
    )
    (basis_rows,) = placed(
        rows_kernel,
        after(place, own_b, cov_got_up, cov_got_down),
        (1,),
        [whole(basis_four.shape)] * 2,
        [shape_of(4, 2, 2 * rows, 2 * cols)],
        (basis_four, basis_x_lo),
    )
    basis_rows = basis_rows.reshape(width, 2 * cols)
    basis_all = lax.all_gather(basis_rows, "factor", axis=0, axis_index_groups=SAME_XHI)
    squares_in, squares_out = placed(
        squares_kernel,
        place,
        (1,),
        [pl.BlockSpec((tokens, width), lambda i, p: (0, p[2])), whole((tokens, width))]
        + [whole((1, tokens))] * 2
        + [whole((width, 2 * cols))]
        + [whole((width, tokens))] * 2,
        [shape_of(1, 2 * cols, dtype=f32), shape_of(5, wide, dtype=f32)],
        (activations, act_got, marks, marks_got, basis_rows, eigen, eigen_got),
    )
    y = fac % 4

    def pair_y(own, got, first):
        return jnp.where(first, jnp.concatenate([own, got], 0), jnp.concatenate([got, own], 0))

    by_y = pair_y(squares_in, lax.ppermute(squares_in, "factor", swap_y(1)), y % 2 == 0)
    by_y = pair_y(by_y, lax.ppermute(by_y, "factor", swap_y(2)), y < 2)
    small = jnp.concatenate([squares_out[:4], by_y, squares_out[4:]], 0)
    give, up, down = lax.optimization_barrier((give, up, down, basis_x_lo))[:3]
    got_a = lax.ppermute(give, "dp", XLO)
    got_up, got_down = send_z(up, down)
    part = chunk // 2
    second_up, second_down, a_first_1, a_second_3, own_a = pl.pallas_call(
        second_kernel,
        out_shape=(
            shape_of(chunk, width),
            shape_of(chunk, width),
            shape_of(part, cut),
            shape_of(part, cut),
            shape_of(2, part, cut),
        ),
        compiler_params=PARAMS,
        name="second_kernel",
    )(after(keep, by_y), got_a, got_up, got_down, first_1, second_3)
    second_got_up, second_got_down = send_z(second_up, second_down)

    small = after(small, second_up)
    small = small + lax.ppermute(small, "dp", XLO)
    small = added(small, *[lax.ppermute(small, "dp", to_z(i)) for i in (1, 3, 2)])
    scale_own = lax.dynamic_index_in_dim(scale_in, core, 0, keepdims=False).reshape(2, 4, cols)
    scale_own = jnp.where(fac // 4 == 0, scale_own, scale_own[::-1])
    scale_own = jnp.concatenate([scale_own[0], scale_own[1]], 1)
    scale_own, scale_chip = lax.optimization_barrier((scale_own, scale_out.reshape(4, wide), second_up))[:2]

    near = pl.BlockSpec((1, chunk, width - cut), lambda i, p: (1, 0, 0))
    third_in = (second_got_up, second_got_down, own_b, a_first_1, a_second_3, own_a)
    third_up, third_down, b_give, b_keep, a_keep = placed(
        third_kernel,
        after(place, small, scale_own, scale_chip),
        (1,),
        [near, near] + [whole(t.shape) for t in third_in],
        [
            shape_of(part, cut),
            shape_of(part, cut),
            shape_of(chunk, width - cut),
            shape_of(chunk, width - cut, dtype=f32),
            shape_of(2, part, cut, dtype=f32),
        ],
        (got_up, got_down, *third_in),
    )
    b_got = lax.ppermute(b_give, "dp", XLO)
    a_via_up, a_via_down = send_z(third_up, third_down)

    healthy_rows = f32(tokens * lax.axis_size("dp")) - small[8, 0]

    cov_next = forward_z(cov_got_up, cov_got_down, cov_rest[2], cov_rest[3])
    cov_next = lax.optimization_barrier((*cov_next, b_got, a_via_up, a_via_down))[:2]
    cov_via_up, cov_via_down = send_z(*cov_next)

    turn_in = (a_keep, a_via_up, a_via_down, b_keep, b_got)
    (turned,) = placed(
        functools.partial(turn_kernel, rows_all=float(tokens * lax.axis_size("dp"))),
        place,
        (4,),
        [whole(t.shape) for t in turn_in]
        + [pl.BlockSpec((1, width, 2 * cols), lambda i, p: (i, 0, 0))]
        + [whole((9, wide)), whole((4, wide)), whole((4, wide))],
        [shape_of(width, chunk)],
        (*turn_in, basis_all, small, scale_own, scale_chip),
        scratch=[
            pltpu.VMEM((chunk, width), bf16),
            pltpu.VMEM((width, chunk), f32),
            pltpu.VMEM((chunk, 128), f32),
        ],
        name="turn_kernel",
    )
    cov_rest = after(cov_rest, turned)
    cov_first = added(cov_rest[0], cov_got_down[1], cov_via_up)
    cov_second = added(cov_rest[1], cov_got_up[1], cov_via_down)
    cov_give = jnp.where(x == 0, cov_second, cov_first).astype(bf16)
    cov_keep = jnp.where(x == 0, cov_first, cov_second)
    cov_sum = added(cov_keep, lax.ppermute(cov_give, "dp", XLO))
    sum_out = cov_sum[:, :width]
    sum_in = cov_sum[:, width:].reshape(rows, 2, cols)
    in_keep = lax.dynamic_index_in_dim(sum_in, core, 1, keepdims=False)
    in_give = lax.dynamic_index_in_dim(sum_in, 1 - core, 1, keepdims=False).astype(bf16)
    in_got = lax.ppermute(in_give, "dp", CORE).astype(f32)

    spread = lax.all_to_all(turned.reshape(16, rows, chunk), "dp", split_axis=0, concat_axis=0)
    result = pl.pallas_call(
        last_kernel, out_shape=shape_of(2, rows, width), compiler_params=PARAMS, name="last_kernel"
    )(spread, basis_out)

    sum_in = jnp.where(core == 0, jnp.stack([in_keep, in_got], 1), jnp.stack([in_got, in_keep], 1))
    new_factor_in = decay_rate * factor_in + blend_weight * sum_in / healthy_rows
    new_factor_out = decay_rate * factor_out + blend_weight * sum_out / healthy_rows
    return (jnp.swapaxes(result, 0, 1), new_factor_in, new_factor_out)


def solution(mesh):
    in_specs = (
        P("dp", None),
        P("dp", "factor"),
        P("dp", None, "factor"),
        P("factor", None),
        P("dp", None, "factor"),
        P("dp", "factor"),
        P(),
        P("factor"),
        P("dp"),
    )
    out_specs = (P("dp", None, "factor"), P("dp", None, "factor"), P("dp", "factor"))
    return jax.shard_map(
        per_device, mesh=mesh, in_specs=in_specs, out_specs=out_specs, check_vma=False
    )
```

```python
import functools

import jax
import jax.numpy as jnp
from jax import lax
from jax.experimental import pallas as pl
from jax.experimental.pallas import tpu as pltpu
from jax.sharding import PartitionSpec as P

decay_rate = 0.9
damping = 0.001
blend_weight = 1.0 - decay_rate

f32 = jnp.float32
bf16 = jnp.bfloat16

CORE = [(i, i ^ 1) for i in range(16)]
XLO = [(i, i ^ 2) for i in range(16)]
XHI = [(j, j ^ 4) for j in range(8)]
SAME_XHI = [[0, 1, 2, 3], [4, 5, 6, 7]]
PARAMS = pltpu.CompilerParams(vmem_limit_bytes=64 * 2**20)


def to_z(s):
    return [(i, ((i >> 2) + s) % 4 * 4 + (i & 3)) for i in range(16)]


def swap_z(bits):
    return [(i, i ^ (bits * 4)) for i in range(16)]


def swap_y(bits):
    return [(j, j ^ bits) for j in range(8)]


UP, DOWN = to_z(1), to_z(3)


def dot(a, b, contract=((1,), (0,)), **kwargs):
    return lax.dot_general(a, b, (contract, ((), ())), preferred_element_type=f32, **kwargs)


def added(*parts):
    total = parts[0].astype(f32)
    for part in parts[1:]:
        total = total + part.astype(f32)
    return total


def after(value, *others):
    return lax.optimization_barrier((value, *others))[0]


def send_z(up, down):
    return lax.ppermute(up, "dp", UP), lax.ppermute(down, "dp", DOWN)


def forward_z(got_up, got_down, first_1, second_3):
    return added(first_1, got_up[0]).astype(bf16), added(second_3, got_down[0]).astype(bf16)


def shape_of(*dims, dtype=bf16):
    return jax.ShapeDtypeStruct(dims, dtype)


def whole(shape):
    return pl.BlockSpec(shape, lambda *_: (0,) * len(shape))


def placed(kernel, place, grid, in_specs, out_shapes, operands, out_specs=None, scratch=(), name=None):
    return pl.pallas_call(
        kernel,
        out_shape=out_shapes,
        grid_spec=pltpu.PrefetchScalarGridSpec(
            num_scalar_prefetch=1,
            grid=grid,
            in_specs=in_specs,
            out_specs=out_specs or [whole(s.shape) for s in out_shapes],
            scratch_shapes=list(scratch),
        ),
        compiler_params=PARAMS,
        name=name or kernel.__name__,
    )(place, *operands)


def healthy(marks):
    return (marks[...] == 0).astype(f32)


def rotate_kernel(place, cot, marks, basis, *refs):
    refs[-1][...] = jnp.swapaxes(dot(cot[...], basis[...]).astype(bf16), 0, 1) * healthy(marks).astype(bf16)


def grad_kernel(place, eigen_0, eigen_1, act_0, act_1, give, keep, up, down, first_1, second_3, own, total):
    chunk, cut = give.shape[1], give.shape[2]
    total[...] = dot(eigen_0[...], act_0[...]) + dot(eigen_1[...], act_1[...])
    outs = ((own, 0, own, 1), (first_1, None, up, 1), (up, 0, down, 0), (down, 1, second_3, None))
    for s in range(4):
        base = (place[0] + s) % 4 * 2 * chunk
        mine = pl.ds(pl.multiple_of(base + place[1] * chunk, 16), chunk)
        other = pl.ds(pl.multiple_of(base + (1 - place[1]) * chunk, 16), chunk)
        give[s] = total[other, :cut].astype(bf16)
        keep[s] = total[mine, :cut].astype(bf16)
        for half in range(2):
            out, at = outs[s][2 * half : 2 * half + 2]
            value = total[pl.ds(pl.multiple_of(base + half * chunk, 16), chunk), cut:].astype(bf16)
            if at is None:
                out[...] = value
            else:
                out[at] = value


def second_kernel(keep, got_a, got_up, got_down, first_1, second_3, up, down, a_first_1, a_second_3, own_a):
    part = own_a.shape[1]
    rest = first_1.shape[1]
    up[:, :rest] = added(first_1[...], got_up[0]).astype(bf16)
    down[:, :rest] = added(second_3[...], got_down[0]).astype(bf16)

    def a_sum(s, half):
        rows = slice(half * part, (half + 1) * part)
        return added(keep[s, rows], got_a[s, rows]).astype(bf16)

    up[:part, rest:] = a_sum(2, 0)
    up[part:, rest:] = a_sum(1, 1)
    down[:part, rest:] = a_sum(2, 1)
    down[part:, rest:] = a_sum(3, 0)
    a_first_1[...] = a_sum(1, 0)
    a_second_3[...] = a_sum(3, 1)
    own_a[0] = a_sum(0, 0)
    own_a[1] = a_sum(0, 1)


def third_kernel(
    place, got_up, got_down, up, down, own_b, a_first_1, a_second_3, own_a, a_up, a_down, give, keep_b, keep_a
):
    part = own_a.shape[1]
    rest = own_b.shape[2]
    a_up[...] = added(a_first_1[...], up[:part, rest:]).astype(bf16)
    a_down[...] = added(a_second_3[...], down[:part, rest:]).astype(bf16)
    first = added(own_b[0], got_down[0], up[:, :rest])
    second = added(own_b[1], got_up[0], down[:, :rest])
    left = place[1] == 0
    give[...] = jnp.where(left, second, first).astype(bf16)
    keep_b[...] = jnp.where(left, first, second)
    keep_a[0] = added(own_a[0], down[part:, rest:])
    keep_a[1] = added(own_a[1], up[part:, rest:])


def cov_kernel(
    place, cot_0, cot_1, marks_0, marks_1, act_0, act_1, cols_0, cols_1, up, down, rest, turned, mine, cov_out, cov_in
):
    places = ((rest, 0, rest, 1), (rest, 2, up, 1), (up, 0, down, 0), (down, 1, rest, 3))
    tokens = cot_0.shape[0]
    rows = mine.shape[0] // 8
    mask_0, mask_1 = healthy(marks_0).astype(bf16), healthy(marks_1).astype(bf16)
    turned[:, :tokens] = jnp.swapaxes(cot_0[...], 0, 1) * mask_0
    turned[:, tokens:] = jnp.swapaxes(cot_1[...], 0, 1) * mask_1
    for s in range(4):
        for x in range(2):
            base = ((place[0] + s) % 4 * 4 + 2 * x + place[2]) * rows
            at = (2 * s + x) * rows
            mine[at : at + rows] = turned[pl.ds(pl.multiple_of(base, 16), rows), :]
    cov_out[...] = dot(mine[:, :tokens], cot_0[...]) + dot(mine[:, tokens:], cot_1[...])
    odd = place[3] % 2
    side = 0.0
    for cols, mask, act in ((cols_0, mask_0, act_0), (cols_1, mask_1, act_1)):
        own = jnp.where(odd == 0, cols[:, : 2 * rows].astype(f32), cols[:, 2 * rows :].astype(f32)).astype(bf16)
        side += dot(jnp.swapaxes(own, 0, 1) * mask, act[...])
    cov_in[...] = jnp.swapaxes(side, 0, 1)
    for s in range(4):
        for x in range(2):
            base = ((place[0] + s) % 4 * 4 + 2 * x) * rows
            pair = [cov_in[pl.ds(pl.multiple_of(base + k * rows, 16), rows), :] for k in range(2)]
            at = (2 * s + x) * rows
            out, index = places[s][2 * x : 2 * x + 2]
            out[index] = jnp.concatenate([cov_out[at : at + rows], *pair], 1).astype(bf16)


def squares_kernel(place, act_0, act_1, marks_0, marks_1, basis, eigen_0, eigen_1, out_in, out_out):
    total = 0.0
    for act, marks in ((act_0, marks_0), (act_1, marks_1)):
        tokens, columns = act.shape[0], basis.shape[1]
        lanes = min(128, columns)
        square = jnp.square(dot(act[...], basis[...]).astype(bf16).astype(f32))
        mask = jnp.swapaxes(jnp.broadcast_to(healthy(marks), (lanes, tokens)), 0, 1)
        total += jnp.sum(square * jnp.concatenate([mask] * (columns // lanes), 1), axis=0, keepdims=True)
    out_in[...] = total
    width, tokens = eigen_0.shape
    lanes = min(128, tokens)
    count = jnp.sum(2.0 - healthy(marks_0) - healthy(marks_1), axis=1, keepdims=True)
    out_out[4:5, :] = jnp.broadcast_to(count, (1, width // 4))
    for at in range(0, width, width // 4):
        rows = slice(at, at + width // 4)
        square = jnp.square(eigen_0[rows].astype(f32)) + jnp.square(eigen_1[rows].astype(f32))
        square = sum(square[:, i : i + lanes] for i in range(0, tokens, lanes))
        out_out[at // (width // 4) : at // (width // 4) + 1, :] = jnp.sum(jnp.swapaxes(square, 0, 1), axis=0, keepdims=True)


def rows_kernel(place, own, got, out):
    for s in range(4):
        out[(place[0] + s) % 4, place[1]] = own[s]
        out[(place[0] + s) % 4, 1 - place[1]] = got[s]


def turn_kernel(
    place, keep_a, via_up, via_down, keep_b, got_b, basis, small, scale_in, scale_out, out, grad, total, lam_out, rows_all
):
    y = pl.program_id(0)
    cut = keep_a.shape[2]
    part = keep_a.shape[1]
    chunk = 2 * part
    healthy_rows = rows_all - small[8:9, 0:1]

    @pl.when(y == 0)
    def _():
        grad[:part, :cut] = added(keep_a[0], via_up[...]).astype(bf16)
        grad[part:, :cut] = added(keep_a[1], via_down[...]).astype(bf16)
        grad[:, cut:] = added(keep_b[...], got_b[...]).astype(bf16)
        total[...] = jnp.zeros(total.shape, f32)
        lam = decay_rate * scale_out[pl.ds(place[0], 1), :] + blend_weight * small[pl.ds(place[0], 1), :] / healthy_rows
        lam = jnp.where(place[1] == 0, lam[:, :chunk], lam[:, chunk:]) * healthy_rows
        lam_out[...] = jnp.swapaxes(jnp.broadcast_to(lam, (lam_out.shape[1], chunk)), 0, 1)

    lam_in = decay_rate * scale_in[pl.ds(y, 1), :] + blend_weight * small[pl.ds(4 + y, 1), :] / healthy_rows
    rotated = dot(grad[...], basis[0])
    scaled = (rotated / (lam_out[:, :1] * lam_in + damping * healthy_rows)).astype(bf16)
    total[...] += dot(basis[0], scaled, ((1,), (1,)))

    @pl.when(y == 3)
    def _():
        rows, main = out.shape[1] * 2 // 3, out.shape[2]
        for d in range(16):
            block = total[d * rows : (d + 1) * rows, :]
            out[d, :rows, :] = block[:, :main].astype(bf16)
            side = block[:, main:]
            out[d, rows:, :] = jnp.concatenate([side[: rows // 2], side[rows // 2 :]], 1).astype(bf16)


def last_kernel(spread, basis_out, out, total):
    z = pl.program_id(0)
    rows, main = out.shape[1], spread.shape[2]

    def block(at):
        side = spread[at, rows:, :]
        side = jnp.concatenate([side[:, : main // 2], side[:, main // 2 :]], 0)
        return jnp.concatenate([spread[at, :rows, :], side], 1)

    lhs = [jnp.concatenate([block(4 * z + a), block(4 * z + 2 + a)], 1) for a in range(2)]
    part = dot(jnp.concatenate(lhs, 0), basis_out[...], ((1,), (1,)))

    @pl.when(z == 0)
    def _():
        total[...] = part

    @pl.when(z > 0)
    def _():
        total[...] += part

    @pl.when(z == 3)
    def _():
        out[0] = total[:rows].astype(bf16)
        out[1] = total[rows:].astype(bf16)


def per_device(
    activations,
    cotangents,
    basis_in,
    basis_out,
    factor_in,
    factor_out,
    scale_in,
    scale_out,
    overflow,
):
    tokens = activations.shape[0]
    width = scale_in.shape[1]
    rows = factor_in.shape[0]
    cols = factor_in.shape[2]
    chunk = width // 8
    wide = width // 4
    cut = width // 3
    dp = lax.axis_index("dp")
    fac = lax.axis_index("factor")
    core, x, z = dp % 2, (dp // 2) % 2, dp // 4
    place = jnp.stack([z, x, core, fac]).astype(jnp.int32)

    basis_keep = lax.dynamic_index_in_dim(basis_in, core, 1, keepdims=False)
    basis_give = lax.dynamic_index_in_dim(basis_in, 1 - core, 1, keepdims=False)
    basis_got = lax.ppermute(basis_give, "dp", CORE)
    marks = overflow.reshape(1, tokens)
    marks_got = lax.ppermute(marks, "dp", CORE)
    cot_got = lax.ppermute(cotangents, "dp", CORE)
    act_give = lax.dynamic_slice_in_dim(activations, (1 - core) * width, width, 1)
    act_got = lax.ppermute(act_give, "dp", CORE)

    def rotate(place, at, before):
        return pl.pallas_call(
            rotate_kernel,
            out_shape=shape_of(width, tokens),
            grid_spec=pltpu.PrefetchScalarGridSpec(
                num_scalar_prefetch=1,
                grid=(2,),
                in_specs=[
                    whole((tokens, width)),
                    whole((1, tokens)),
                    pl.BlockSpec((width, wide), lambda i, p: (0, at + i)),
                ]
                + [pl.BlockSpec(memory_space=pl.ANY)] * len(before),
                out_specs=pl.BlockSpec((wide, tokens), lambda i, p: (at + i, 0)),
            ),
            input_output_aliases={4: 0} if before else {},
            compiler_params=PARAMS,
            name="rotate_kernel",
        )(place, cotangents, marks, basis_out, *before)

    eigen_half = rotate(after(place, act_give, basis_give), 0, ())
    basis_mine = after(basis_keep, eigen_half)
    basis_chip = jnp.where(
        core == 0,
        jnp.concatenate([basis_mine, basis_got], 0),
        jnp.concatenate([basis_got, basis_mine], 0),
    )
    basis_x_hi = lax.ppermute(basis_chip, "factor", XHI)
    eigen = rotate(after(place, basis_chip, marks_got), 2, (eigen_half,))
    eigen_got = lax.ppermute(after(eigen, basis_x_hi), "dp", CORE)
    basis_pair = jnp.concatenate([after(basis_chip, eigen), basis_x_hi], 1)
    basis_z = [lax.ppermute(basis_pair, "dp", to_z(4 - s)) for s in (1, 2, 3)]

    def own_block(n, at):
        return pl.BlockSpec((tokens, n), lambda i, p: (0, at(i, p)))

    columns = width + 2 * cols
    cov_up, cov_down, cov_rest = placed(
        cov_kernel,
        after(place, basis_pair),
        (1,),
        [whole((tokens, width))] * 2
        + [whole((1, tokens))] * 2
        + [own_block(width, lambda i, p: p[2]), whole((tokens, width))]
        + [own_block(wide, lambda i, p: p[2] * 4 + p[3] // 2), own_block(wide, lambda i, p: p[3] // 2)],
        [shape_of(n, rows, columns) for n in (2, 2, 4)],
        (cotangents, cot_got, marks, marks_got, activations, act_got, activations, act_got),
        scratch=[
            pltpu.VMEM((width, 2 * tokens), bf16),
            pltpu.VMEM((8 * rows, 2 * tokens), bf16),
            pltpu.VMEM((8 * rows, width), f32),
            pltpu.VMEM((width, cols), f32),
        ],
    )
    cov_got_up, cov_got_down = send_z(cov_up, cov_down)

    basis_four = jnp.stack([after(basis_pair, cov_up), *basis_z])
    basis_x_lo = lax.ppermute(basis_four, "dp", XLO)

    single = shape_of(chunk, width - cut)
    pair = shape_of(2, chunk, width - cut)
    four = shape_of(4, chunk, cut)
    give, keep, up, down, first_1, second_3, own_b = placed(
        grad_kernel,
        after(place, basis_four),
        (1,),
        [whole((width, tokens))] * 2
        + [pl.BlockSpec((tokens, width), lambda i, p: (0, p[2])), whole((tokens, width))],
        [four, four, pair, pair, single, single, pair],
        (eigen, eigen_got, activations, act_got),
        scratch=[pltpu.VMEM((width, width), f32)],
    )
    (basis_rows,) = placed(
        rows_kernel,
        after(place, own_b, cov_got_up, cov_got_down),
        (1,),
        [whole(basis_four.shape)] * 2,
        [shape_of(4, 2, 2 * rows, 2 * cols)],
        (basis_four, basis_x_lo),
    )
    basis_rows = basis_rows.reshape(width, 2 * cols)
    basis_all = lax.all_gather(basis_rows, "factor", axis=0, axis_index_groups=SAME_XHI)
    squares_in, squares_out = placed(
        squares_kernel,
        place,
        (1,),
        [pl.BlockSpec((tokens, width), lambda i, p: (0, p[2])), whole((tokens, width))]
        + [whole((1, tokens))] * 2
        + [whole((width, 2 * cols))]
        + [whole((width, tokens))] * 2,
        [shape_of(1, 2 * cols, dtype=f32), shape_of(5, wide, dtype=f32)],
        (activations, act_got, marks, marks_got, basis_rows, eigen, eigen_got),
    )
    y = fac % 4

    def pair_y(own, got, first):
        return jnp.where(first, jnp.concatenate([own, got], 0), jnp.concatenate([got, own], 0))

    by_y = pair_y(squares_in, lax.ppermute(squares_in, "factor", swap_y(1)), y % 2 == 0)
    by_y = pair_y(by_y, lax.ppermute(by_y, "factor", swap_y(2)), y < 2)
    small = jnp.concatenate([squares_out[:4], by_y, squares_out[4:]], 0)
    give, up, down = lax.optimization_barrier((give, up, down, basis_x_lo))[:3]
    got_a = lax.ppermute(give, "dp", XLO)
    got_up, got_down = send_z(up, down)
    part = chunk // 2
    second_up, second_down, a_first_1, a_second_3, own_a = pl.pallas_call(
        second_kernel,
        out_shape=(
            shape_of(chunk, width),
            shape_of(chunk, width),
            shape_of(part, cut),
            shape_of(part, cut),
            shape_of(2, part, cut),
        ),
        compiler_params=PARAMS,
        name="second_kernel",
    )(after(keep, by_y), got_a, got_up, got_down, first_1, second_3)
    second_got_up, second_got_down = send_z(second_up, second_down)

    small = after(small, second_up)
    small = small + lax.ppermute(small, "dp", XLO)
    small = added(small, *[lax.ppermute(small, "dp", to_z(i)) for i in (1, 3, 2)])
    scale_own = lax.dynamic_index_in_dim(scale_in, core, 0, keepdims=False).reshape(2, 4, cols)
    scale_own = jnp.where(fac // 4 == 0, scale_own, scale_own[::-1])
    scale_own = jnp.concatenate([scale_own[0], scale_own[1]], 1)
    scale_own, scale_chip = lax.optimization_barrier((scale_own, scale_out.reshape(4, wide), second_up))[:2]

    near = pl.BlockSpec((1, chunk, width - cut), lambda i, p: (1, 0, 0))
    third_in = (second_got_up, second_got_down, own_b, a_first_1, a_second_3, own_a)
    third_up, third_down, b_give, b_keep, a_keep = placed(
        third_kernel,
        after(place, small, scale_own, scale_chip),
        (1,),
        [near, near] + [whole(t.shape) for t in third_in],
        [
            shape_of(part, cut),
            shape_of(part, cut),
            shape_of(chunk, width - cut),
            shape_of(chunk, width - cut, dtype=f32),
            shape_of(2, part, cut, dtype=f32),
        ],
        (got_up, got_down, *third_in),
    )
    b_got = lax.ppermute(b_give, "dp", XLO)
    a_via_up, a_via_down = send_z(third_up, third_down)

    healthy_rows = f32(tokens * lax.axis_size("dp")) - small[8, 0]

    cov_next = forward_z(cov_got_up, cov_got_down, cov_rest[2], cov_rest[3])
    cov_next = lax.optimization_barrier((*cov_next, b_got, a_via_up, a_via_down, healthy_rows))[:2]
    cov_via_up, cov_via_down = send_z(*cov_next)

    turn_in = (a_keep, a_via_up, a_via_down, b_keep, b_got)
    (turned,) = placed(
        functools.partial(turn_kernel, rows_all=float(tokens * lax.axis_size("dp"))),
        place,
        (4,),
        [whole(t.shape) for t in turn_in]
        + [pl.BlockSpec((1, width, 2 * cols), lambda i, p: (i, 0, 0))]
        + [whole((9, wide)), whole((4, wide)), whole((4, wide))],
        [shape_of(16, rows * 3 // 2, chunk * 2 // 3)],
        (*turn_in, basis_all, small, scale_own, scale_chip),
        scratch=[
            pltpu.VMEM((chunk, width), bf16),
            pltpu.VMEM((width, chunk), f32),
            pltpu.VMEM((chunk, 128), f32),
        ],
        name="turn_kernel",
    )
    cov_rest = after(cov_rest, turned)
    cov_first = added(cov_rest[0], cov_got_down[1], cov_via_up)
    cov_second = added(cov_rest[1], cov_got_up[1], cov_via_down)
    cov_give = jnp.where(x == 0, cov_second, cov_first).astype(bf16)
    cov_keep = jnp.where(x == 0, cov_first, cov_second)
    cov_sum = added(cov_keep, lax.ppermute(cov_give, "dp", XLO))
    sum_out = cov_sum[:, :width]
    sum_in = cov_sum[:, width:].reshape(rows, 2, cols)
    in_keep = lax.dynamic_index_in_dim(sum_in, core, 1, keepdims=False)
    in_give = lax.dynamic_index_in_dim(sum_in, 1 - core, 1, keepdims=False).astype(bf16)
    in_got = lax.ppermute(in_give, "dp", CORE).astype(f32)

    spread = lax.all_to_all(turned, "dp", split_axis=0, concat_axis=0)
    result = pl.pallas_call(
        last_kernel,
        out_shape=shape_of(2, rows, width),
        grid=(4,),
        in_specs=[whole(spread.shape), pl.BlockSpec((width, wide), lambda i: (0, i))],
        out_specs=whole((2, rows, width)),
        scratch_shapes=[pltpu.VMEM((2 * rows, width), f32)],
        compiler_params=PARAMS,
        name="last_kernel",
    )(spread, basis_out)

    sum_in = jnp.where(core == 0, jnp.stack([in_keep, in_got], 1), jnp.stack([in_got, in_keep], 1))
    new_factor_in = decay_rate * factor_in + blend_weight * sum_in / healthy_rows
    new_factor_out = decay_rate * factor_out + blend_weight * sum_out / healthy_rows
    return (jnp.swapaxes(result, 0, 1), new_factor_in, new_factor_out)


def solution(mesh):
    in_specs = (
        P("dp", None),
        P("dp", "factor"),
        P("dp", None, "factor"),
        P("factor", None),
        P("dp", None, "factor"),
        P("dp", "factor"),
        P(),
        P("factor"),
        P("dp"),
    )
    out_specs = (P("dp", None, "factor"), P("dp", None, "factor"), P("dp", "factor"))
    return jax.shard_map(
        per_device, mesh=mesh, in_specs=in_specs, out_specs=out_specs, check_vma=False
    )
```

```python
import functools

import jax
import jax.numpy as jnp
from jax import lax
from jax.experimental import pallas as pl
from jax.experimental.pallas import tpu as pltpu
from jax.sharding import PartitionSpec as P

decay_rate = 0.9
damping = 0.001
blend_weight = 1.0 - decay_rate

f32 = jnp.float32
bf16 = jnp.bfloat16

CORE = [(i, i ^ 1) for i in range(16)]
XLO = [(i, i ^ 2) for i in range(16)]
XHI = [(j, j ^ 4) for j in range(8)]
SAME_XHI = [[0, 1, 2, 3], [4, 5, 6, 7]]
PARAMS = pltpu.CompilerParams(vmem_limit_bytes=64 * 2**20)
EARLY = pltpu.CompilerParams(vmem_limit_bytes=56 * 2**20)


def to_z(s):
    return [(i, ((i >> 2) + s) % 4 * 4 + (i & 3)) for i in range(16)]


def swap_z(bits):
    return [(i, i ^ (bits * 4)) for i in range(16)]


def swap_y(bits):
    return [(j, j ^ bits) for j in range(8)]


UP, DOWN = to_z(1), to_z(3)


def dot(a, b, contract=((1,), (0,)), **kwargs):
    return lax.dot_general(a, b, (contract, ((), ())), preferred_element_type=f32, **kwargs)


def added(*parts):
    total = parts[0].astype(f32)
    for part in parts[1:]:
        total = total + part.astype(f32)
    return total


def after(value, *others):
    return lax.optimization_barrier((value, *others))[0]


def send_z(up, down):
    return lax.ppermute(up, "dp", UP), lax.ppermute(down, "dp", DOWN)


def forward_z(got_up, got_down, first_1, second_3):
    return added(first_1, got_up[0]).astype(bf16), added(second_3, got_down[0]).astype(bf16)


def shape_of(*dims, dtype=bf16):
    return jax.ShapeDtypeStruct(dims, dtype)


def whole(shape):
    return pl.BlockSpec(shape, lambda *_: (0,) * len(shape))


def placed(kernel, place, grid, in_specs, out_shapes, operands, out_specs=None, scratch=(), name=None, params=PARAMS):
    return pl.pallas_call(
        kernel,
        out_shape=out_shapes,
        grid_spec=pltpu.PrefetchScalarGridSpec(
            num_scalar_prefetch=1,
            grid=grid,
            in_specs=in_specs,
            out_specs=out_specs or [whole(s.shape) for s in out_shapes],
            scratch_shapes=list(scratch),
        ),
        compiler_params=params,
        name=name or kernel.__name__,
    )(place, *operands)


def healthy(marks):
    return (marks[...] == 0).astype(f32)


def rotate_kernel(place, cot, marks, basis, *refs):
    refs[-1][...] = jnp.swapaxes(dot(cot[...], basis[...]).astype(bf16), 0, 1) * healthy(marks).astype(bf16)


def grad_kernel(place, eigen_0, eigen_1, act_0, act_1, give, keep, up, down, first_1, second_3, own, total):
    chunk, cut = give.shape[1], give.shape[2]
    total[...] = dot(eigen_0[...], act_0[...]) + dot(eigen_1[...], act_1[...])
    outs = ((own, 0, own, 1), (first_1, None, up, 1), (up, 0, down, 0), (down, 1, second_3, None))
    for s in range(4):
        base = (place[0] + s) % 4 * 2 * chunk
        mine = pl.ds(pl.multiple_of(base + place[1] * chunk, 16), chunk)
        other = pl.ds(pl.multiple_of(base + (1 - place[1]) * chunk, 16), chunk)
        give[s] = total[other, :cut].astype(bf16)
        keep[s] = total[mine, :cut].astype(bf16)
        for half in range(2):
            out, at = outs[s][2 * half : 2 * half + 2]
            value = total[pl.ds(pl.multiple_of(base + half * chunk, 16), chunk), cut:].astype(bf16)
            if at is None:
                out[...] = value
            else:
                out[at] = value


def second_kernel(keep, got_a, got_up, got_down, first_1, second_3, up, down, a_first_1, a_second_3, own_a):
    part = own_a.shape[1]
    rest = first_1.shape[1]
    up[:, :rest] = added(first_1[...], got_up[0]).astype(bf16)
    down[:, :rest] = added(second_3[...], got_down[0]).astype(bf16)

    def a_sum(s, half):
        rows = slice(half * part, (half + 1) * part)
        return added(keep[s, rows], got_a[s, rows]).astype(bf16)

    up[:part, rest:] = a_sum(2, 0)
    up[part:, rest:] = a_sum(1, 1)
    down[:part, rest:] = a_sum(2, 1)
    down[part:, rest:] = a_sum(3, 0)
    a_first_1[...] = a_sum(1, 0)
    a_second_3[...] = a_sum(3, 1)
    own_a[0] = a_sum(0, 0)
    own_a[1] = a_sum(0, 1)


def third_kernel(
    place, got_up, got_down, up, down, own_b, a_first_1, a_second_3, own_a, a_up, a_down, give, keep_b, keep_a
):
    part = own_a.shape[1]
    rest = own_b.shape[2]
    a_up[...] = added(a_first_1[...], up[:part, rest:]).astype(bf16)
    a_down[...] = added(a_second_3[...], down[:part, rest:]).astype(bf16)
    first = added(own_b[0], got_down[0], up[:, :rest])
    second = added(own_b[1], got_up[0], down[:, :rest])
    left = place[1] == 0
    give[...] = jnp.where(left, second, first).astype(bf16)
    keep_b[...] = jnp.where(left, first, second)
    keep_a[0] = added(own_a[0], down[part:, rest:])
    keep_a[1] = added(own_a[1], up[part:, rest:])


def cov_kernel(
    place, cot_0, cot_1, marks_0, marks_1, act_0, act_1, cols_0, cols_1, up, down, rest, turned, mine, cov_out, cov_in
):
    places = ((rest, 0, rest, 1), (rest, 2, up, 1), (up, 0, down, 0), (down, 1, rest, 3))
    tokens = cot_0.shape[0]
    rows = mine.shape[0] // 8
    mask_0, mask_1 = healthy(marks_0).astype(bf16), healthy(marks_1).astype(bf16)
    turned[:, :tokens] = jnp.swapaxes(cot_0[...], 0, 1) * mask_0
    turned[:, tokens:] = jnp.swapaxes(cot_1[...], 0, 1) * mask_1
    for s in range(4):
        for x in range(2):
            base = ((place[0] + s) % 4 * 4 + 2 * x + place[2]) * rows
            at = (2 * s + x) * rows
            mine[at : at + rows] = turned[pl.ds(pl.multiple_of(base, 16), rows), :]
    cov_out[...] = dot(mine[:, :tokens], cot_0[...]) + dot(mine[:, tokens:], cot_1[...])
    odd = place[3] % 2
    side = 0.0
    for cols, mask, act in ((cols_0, mask_0, act_0), (cols_1, mask_1, act_1)):
        own = jnp.where(odd == 0, cols[:, : 2 * rows].astype(f32), cols[:, 2 * rows :].astype(f32)).astype(bf16)
        side += dot(jnp.swapaxes(own, 0, 1) * mask, act[...])
    cov_in[...] = jnp.swapaxes(side, 0, 1)
    for s in range(4):
        for x in range(2):
            base = ((place[0] + s) % 4 * 4 + 2 * x) * rows
            pair = [cov_in[pl.ds(pl.multiple_of(base + k * rows, 16), rows), :] for k in range(2)]
            at = (2 * s + x) * rows
            out, index = places[s][2 * x : 2 * x + 2]
            out[index] = jnp.concatenate([cov_out[at : at + rows], *pair], 1).astype(bf16)


def squares_kernel(place, act_0, act_1, marks_0, marks_1, basis, eigen_0, eigen_1, out_in, out_out):
    total = 0.0
    for act, marks in ((act_0, marks_0), (act_1, marks_1)):
        tokens, columns = act.shape[0], basis.shape[1]
        lanes = min(128, columns)
        square = jnp.square(dot(act[...], basis[...]).astype(bf16).astype(f32))
        mask = jnp.swapaxes(jnp.broadcast_to(healthy(marks), (lanes, tokens)), 0, 1)
        total += jnp.sum(square * jnp.concatenate([mask] * (columns // lanes), 1), axis=0, keepdims=True)
    out_in[...] = total
    width, tokens = eigen_0.shape
    lanes = min(128, tokens)
    count = jnp.sum(2.0 - healthy(marks_0) - healthy(marks_1), axis=1, keepdims=True)
    out_out[4:5, :] = jnp.broadcast_to(count, (1, width // 4))
    for at in range(0, width, width // 4):
        rows = slice(at, at + width // 4)
        square = jnp.square(eigen_0[rows].astype(f32)) + jnp.square(eigen_1[rows].astype(f32))
        square = sum(square[:, i : i + lanes] for i in range(0, tokens, lanes))
        out_out[at // (width // 4) : at // (width // 4) + 1, :] = jnp.sum(jnp.swapaxes(square, 0, 1), axis=0, keepdims=True)


def rows_kernel(place, own, got, out):
    for s in range(4):
        out[(place[0] + s) % 4, place[1]] = own[s]
        out[(place[0] + s) % 4, 1 - place[1]] = got[s]


def turn_kernel(
    place, keep_a, via_up, via_down, keep_b, got_b, basis, small, scale_in, scale_out, out, grad, total, lam_out, scales, rows_all
):
    y = pl.program_id(0)
    cut = keep_a.shape[2]
    part = keep_a.shape[1]
    chunk = 2 * part
    healthy_rows = rows_all - small[4:5, 0:1]

    @pl.when(y == 0)
    def _():
        grad[:part, :cut] = added(keep_a[0], via_up[...]).astype(bf16)
        grad[part:, :cut] = added(keep_a[1], via_down[...]).astype(bf16)
        grad[:, cut:] = added(keep_b[...], got_b[...]).astype(bf16)
        total[...] = jnp.zeros(total.shape, f32)
        wide = 2 * chunk
        scale = scale_out[:, pl.ds(pl.multiple_of(place[0] * wide, wide), wide)]
        lam = decay_rate * scale + blend_weight * small[pl.ds(place[0], 1), :] / healthy_rows
        lam = jnp.where(place[1] == 0, lam[:, :chunk], lam[:, chunk:]) * healthy_rows
        row = scale_in[pl.ds(place[2], 1), :]
        for k in range(4):
            halves = [row[:, i : i + chunk] for i in (k * chunk, (4 + k) * chunk)]
            swapped = jnp.concatenate(halves[::-1], 1)
            scales[k : k + 1, :] = jnp.where(place[3] < 4, jnp.concatenate(halves, 1), swapped)
        lam_out[...] = jnp.swapaxes(jnp.broadcast_to(lam, (lam_out.shape[1], chunk)), 0, 1)

    lam_in = decay_rate * scales[pl.ds(y, 1), :] + blend_weight * small[pl.ds(5 + y, 1), :] / healthy_rows
    rotated = dot(grad[...], basis[0])
    scaled = (rotated / (lam_out[:, :1] * lam_in + damping * healthy_rows)).astype(bf16)
    total[...] += dot(basis[0], scaled, ((1,), (1,)))

    @pl.when(y == 3)
    def _():
        rows, main = out.shape[1] * 2 // 3, out.shape[2]
        for d in range(16):
            block = total[d * rows : (d + 1) * rows, :]
            out[d, :rows, :] = block[:, :main].astype(bf16)
            side = block[:, main:]
            out[d, rows:, :] = jnp.concatenate([side[: rows // 2], side[rows // 2 :]], 1).astype(bf16)


def last_kernel(spread, basis_out, out, total):
    z = pl.program_id(0)
    rows, main = out.shape[1], spread.shape[2]

    def block(at):
        side = spread[at, rows:, :]
        side = jnp.concatenate([side[:, : main // 2], side[:, main // 2 :]], 0)
        return jnp.concatenate([spread[at, :rows, :], side], 1)

    lhs = [jnp.concatenate([block(4 * z + a), block(4 * z + 2 + a)], 1) for a in range(2)]
    part = dot(jnp.concatenate(lhs, 0), basis_out[...], ((1,), (1,)))

    @pl.when(z == 0)
    def _():
        total[...] = part

    @pl.when(z > 0)
    def _():
        total[...] += part

    @pl.when(z == 3)
    def _():
        out[0] = total[:rows].astype(bf16)
        out[1] = total[rows:].astype(bf16)


def per_device(
    activations,
    cotangents,
    basis_in,
    basis_out,
    factor_in,
    factor_out,
    scale_in,
    scale_out,
    overflow,
):
    tokens = activations.shape[0]
    width = scale_in.shape[1]
    rows = factor_in.shape[0]
    cols = factor_in.shape[2]
    chunk = width // 8
    wide = width // 4
    cut = width // 3
    dp = lax.axis_index("dp")
    fac = lax.axis_index("factor")
    core, x, z = dp % 2, (dp // 2) % 2, dp // 4
    place = jnp.stack([z, x, core, fac]).astype(jnp.int32)

    basis_keep = lax.dynamic_index_in_dim(basis_in, core, 1, keepdims=False)
    basis_give = lax.dynamic_index_in_dim(basis_in, 1 - core, 1, keepdims=False)
    basis_got = lax.ppermute(basis_give, "dp", CORE)
    marks = overflow.reshape(1, tokens)
    marks_got = lax.ppermute(marks, "dp", CORE)
    cot_got = lax.ppermute(cotangents, "dp", CORE)
    act_give = lax.dynamic_slice_in_dim(activations, (1 - core) * width, width, 1)
    act_got = lax.ppermute(act_give, "dp", CORE)

    def rotate(place, at, before):
        return pl.pallas_call(
            rotate_kernel,
            out_shape=shape_of(width, tokens),
            grid_spec=pltpu.PrefetchScalarGridSpec(
                num_scalar_prefetch=1,
                grid=(2,),
                in_specs=[
                    whole((tokens, width)),
                    whole((1, tokens)),
                    pl.BlockSpec((width, wide), lambda i, p: (0, at + i)),
                ]
                + [pl.BlockSpec(memory_space=pl.ANY)] * len(before),
                out_specs=pl.BlockSpec((wide, tokens), lambda i, p: (at + i, 0)),
            ),
            input_output_aliases={4: 0} if before else {},
            compiler_params=EARLY,
            name="rotate_kernel",
        )(place, cotangents, marks, basis_out, *before)

    eigen_half = rotate(after(place, act_give, basis_give), 0, ())
    basis_mine = after(basis_keep, eigen_half)
    basis_chip = jnp.where(
        core == 0,
        jnp.concatenate([basis_mine, basis_got], 0),
        jnp.concatenate([basis_got, basis_mine], 0),
    )
    basis_x_hi = lax.ppermute(basis_chip, "factor", XHI)
    eigen = rotate(after(place, basis_chip, marks_got), 2, (eigen_half,))
    eigen_got = lax.ppermute(after(eigen, basis_x_hi), "dp", CORE)
    basis_pair = jnp.concatenate([after(basis_chip, eigen), basis_x_hi], 1)
    basis_z = [lax.ppermute(basis_pair, "dp", to_z(4 - s)) for s in (1, 2, 3)]

    def own_block(n, at):
        return pl.BlockSpec((tokens, n), lambda i, p: (0, at(i, p)))

    columns = width + 2 * cols
    cov_up, cov_down, cov_rest = placed(
        cov_kernel,
        after(place, basis_pair),
        (1,),
        [whole((tokens, width))] * 2
        + [whole((1, tokens))] * 2
        + [own_block(width, lambda i, p: p[2]), whole((tokens, width))]
        + [own_block(wide, lambda i, p: p[2] * 4 + p[3] // 2), own_block(wide, lambda i, p: p[3] // 2)],
        [shape_of(n, rows, columns) for n in (2, 2, 4)],
        (cotangents, cot_got, marks, marks_got, activations, act_got, activations, act_got),
        scratch=[
            pltpu.VMEM((width, 2 * tokens), bf16),
            pltpu.VMEM((8 * rows, 2 * tokens), bf16),
            pltpu.VMEM((8 * rows, width), f32),
            pltpu.VMEM((width, cols), f32),
        ],
        params=EARLY,
    )
    cov_got_up, cov_got_down = send_z(cov_up, cov_down)

    basis_four = jnp.stack([after(basis_pair, cov_up), *basis_z])
    basis_x_lo = lax.ppermute(basis_four, "dp", XLO)

    single = shape_of(chunk, width - cut)
    pair = shape_of(2, chunk, width - cut)
    four = shape_of(4, chunk, cut)
    give, keep, up, down, first_1, second_3, own_b = placed(
        grad_kernel,
        after(place, basis_four),
        (1,),
        [whole((width, tokens))] * 2
        + [pl.BlockSpec((tokens, width), lambda i, p: (0, p[2])), whole((tokens, width))],
        [four, four, pair, pair, single, single, pair],
        (eigen, eigen_got, activations, act_got),
        scratch=[pltpu.VMEM((width, width), f32)],
    )
    scale_row = after(scale_out, own_b).reshape(1, width)
    (basis_rows,) = placed(
        rows_kernel,
        after(place, own_b, cov_got_up, cov_got_down, scale_row),
        (1,),
        [whole(basis_four.shape)] * 2,
        [shape_of(4, 2, 2 * rows, 2 * cols)],
        (basis_four, basis_x_lo),
    )
    basis_rows = basis_rows.reshape(width, 2 * cols)
    basis_all = lax.all_gather(basis_rows, "factor", axis=0, axis_index_groups=SAME_XHI)
    squares_in, squares_out = placed(
        squares_kernel,
        place,
        (1,),
        [pl.BlockSpec((tokens, width), lambda i, p: (0, p[2])), whole((tokens, width))]
        + [whole((1, tokens))] * 2
        + [whole((width, 2 * cols))]
        + [whole((width, tokens))] * 2,
        [shape_of(1, 2 * cols, dtype=f32), shape_of(5, wide, dtype=f32)],
        (activations, act_got, marks, marks_got, basis_rows, eigen, eigen_got),
    )
    y = fac % 4

    def pair_y(own, got, first):
        return jnp.where(first, jnp.concatenate([own, got], 0), jnp.concatenate([got, own], 0))

    by_y = pair_y(squares_in, lax.ppermute(squares_in, "factor", swap_y(1)), y % 2 == 0)
    by_y = pair_y(by_y, lax.ppermute(by_y, "factor", swap_y(2)), y < 2)
    small = jnp.concatenate([squares_out, by_y], 0)
    give, up, down = lax.optimization_barrier((give, up, down, basis_x_lo))[:3]
    got_a = lax.ppermute(give, "dp", XLO)
    got_up, got_down = send_z(up, down)
    part = chunk // 2
    second_up, second_down, a_first_1, a_second_3, own_a = pl.pallas_call(
        second_kernel,
        out_shape=(
            shape_of(chunk, width),
            shape_of(chunk, width),
            shape_of(part, cut),
            shape_of(part, cut),
            shape_of(2, part, cut),
        ),
        compiler_params=PARAMS,
        name="second_kernel",
    )(after(keep, by_y), got_a, got_up, got_down, first_1, second_3)
    second_got_up, second_got_down = send_z(second_up, second_down)

    small = after(small, second_up)
    small = small + lax.ppermute(small, "dp", XLO)
    small = added(small, *[lax.ppermute(small, "dp", to_z(i)) for i in (1, 3, 2)])
    near = pl.BlockSpec((1, chunk, width - cut), lambda i, p: (1, 0, 0))
    third_in = (second_got_up, second_got_down, own_b, a_first_1, a_second_3, own_a)
    third_up, third_down, b_give, b_keep, a_keep = placed(
        third_kernel,
        after(place, small),
        (1,),
        [near, near] + [whole(t.shape) for t in third_in],
        [
            shape_of(part, cut),
            shape_of(part, cut),
            shape_of(chunk, width - cut),
            shape_of(chunk, width - cut, dtype=f32),
            shape_of(2, part, cut, dtype=f32),
        ],
        (got_up, got_down, *third_in),
    )
    b_got = lax.ppermute(b_give, "dp", XLO)
    a_via_up, a_via_down = send_z(third_up, third_down)

    healthy_rows = f32(tokens * lax.axis_size("dp")) - small[4, 0]

    cov_next = forward_z(cov_got_up, cov_got_down, cov_rest[2], cov_rest[3])
    cov_next = lax.optimization_barrier((*cov_next, b_got, a_via_up, a_via_down, healthy_rows))[:2]
    cov_via_up, cov_via_down = send_z(*cov_next)

    turn_in = (a_keep, a_via_up, a_via_down, b_keep, b_got)
    (turned,) = placed(
        functools.partial(turn_kernel, rows_all=float(tokens * lax.axis_size("dp"))),
        place,
        (4,),
        [whole(t.shape) for t in turn_in]
        + [pl.BlockSpec((1, width, 2 * cols), lambda i, p: (i, 0, 0))]
        + [whole((9, wide)), whole((2, width)), whole((1, width))],
        [shape_of(16, rows * 3 // 2, chunk * 2 // 3)],
        (*turn_in, basis_all, small, scale_in, scale_row),
        scratch=[
            pltpu.VMEM((chunk, width), bf16),
            pltpu.VMEM((width, chunk), f32),
            pltpu.VMEM((chunk, 128), f32),
            pltpu.VMEM((4, wide), f32),
        ],
        name="turn_kernel",
    )
    cov_rest = after(cov_rest, turned)
    cov_first = added(cov_rest[0], cov_got_down[1], cov_via_up)
    cov_second = added(cov_rest[1], cov_got_up[1], cov_via_down)
    cov_give = jnp.where(x == 0, cov_second, cov_first).astype(bf16)
    cov_keep = jnp.where(x == 0, cov_first, cov_second)
    cov_sum = added(cov_keep, lax.ppermute(cov_give, "dp", XLO))
    sum_out = cov_sum[:, :width]
    sum_in = cov_sum[:, width:].reshape(rows, 2, cols)
    in_keep = lax.dynamic_index_in_dim(sum_in, core, 1, keepdims=False)
    in_give = lax.dynamic_index_in_dim(sum_in, 1 - core, 1, keepdims=False).astype(bf16)
    in_got = lax.ppermute(in_give, "dp", CORE).astype(f32)

    spread = lax.all_to_all(turned, "dp", split_axis=0, concat_axis=0)
    result = pl.pallas_call(
        last_kernel,
        out_shape=shape_of(2, rows, width),
        grid=(4,),
        in_specs=[whole(spread.shape), pl.BlockSpec((width, wide), lambda i: (0, i))],
        out_specs=whole((2, rows, width)),
        scratch_shapes=[pltpu.VMEM((2 * rows, width), f32)],
        compiler_params=PARAMS,
        name="last_kernel",
    )(spread, basis_out)

    sum_in = jnp.where(core == 0, jnp.stack([in_keep, in_got], 1), jnp.stack([in_got, in_keep], 1))
    new_factor_in = decay_rate * factor_in + blend_weight * sum_in / healthy_rows
    new_factor_out = decay_rate * factor_out + blend_weight * sum_out / healthy_rows
    return (jnp.swapaxes(result, 0, 1), new_factor_in, new_factor_out)


def solution(mesh):
    in_specs = (
        P("dp", None),
        P("dp", "factor"),
        P("dp", None, "factor"),
        P("factor", None),
        P("dp", None, "factor"),
        P("dp", "factor"),
        P(),
        P("factor"),
        P("dp"),
    )
    out_specs = (P("dp", None, "factor"), P("dp", None, "factor"), P("dp", "factor"))
    return jax.shard_map(
        per_device, mesh=mesh, in_specs=in_specs, out_specs=out_specs, check_vma=False
    )
```

```python
import functools

import jax
import jax.numpy as jnp
from jax import lax
from jax.experimental import pallas as pl
from jax.experimental.pallas import tpu as pltpu
from jax.sharding import PartitionSpec as P

decay_rate = 0.9
damping = 0.001
blend_weight = 1.0 - decay_rate

f32 = jnp.float32
bf16 = jnp.bfloat16

CORE = [(i, i ^ 1) for i in range(16)]
XLO = [(i, i ^ 2) for i in range(16)]
XHI = [(j, j ^ 4) for j in range(8)]
SAME_XHI = [[0, 1, 2, 3], [4, 5, 6, 7]]
PARAMS = pltpu.CompilerParams(vmem_limit_bytes=64 * 2**20)
EARLY = pltpu.CompilerParams(vmem_limit_bytes=56 * 2**20)


def to_z(s):
    return [(i, ((i >> 2) + s) % 4 * 4 + (i & 3)) for i in range(16)]


def swap_z(bits):
    return [(i, i ^ (bits * 4)) for i in range(16)]


def swap_y(bits):
    return [(j, j ^ bits) for j in range(8)]


UP, DOWN = to_z(1), to_z(3)


def dot(a, b, contract=((1,), (0,)), **kwargs):
    return lax.dot_general(a, b, (contract, ((), ())), preferred_element_type=f32, **kwargs)


def added(*parts):
    total = parts[0].astype(f32)
    for part in parts[1:]:
        total = total + part.astype(f32)
    return total


def after(value, *others):
    return lax.optimization_barrier((value, *others))[0]


def send_z(up, down):
    return lax.ppermute(up, "dp", UP), lax.ppermute(down, "dp", DOWN)


def forward_z(got_up, got_down, first_1, second_3):
    return added(first_1, got_up[0]).astype(bf16), added(second_3, got_down[0]).astype(bf16)


def shape_of(*dims, dtype=bf16):
    return jax.ShapeDtypeStruct(dims, dtype)


def whole(shape):
    return pl.BlockSpec(shape, lambda *_: (0,) * len(shape))


def placed(kernel, place, grid, in_specs, out_shapes, operands, out_specs=None, scratch=(), name=None, params=PARAMS):
    return pl.pallas_call(
        kernel,
        out_shape=out_shapes,
        grid_spec=pltpu.PrefetchScalarGridSpec(
            num_scalar_prefetch=1,
            grid=grid,
            in_specs=in_specs,
            out_specs=out_specs or [whole(s.shape) for s in out_shapes],
            scratch_shapes=list(scratch),
        ),
        compiler_params=params,
        name=name or kernel.__name__,
    )(place, *operands)


def healthy(marks):
    return (marks[...] == 0).astype(f32)


def rotate_kernel(place, cot, marks, basis, *refs):
    refs[-1][...] = jnp.swapaxes(dot(cot[...], basis[...]).astype(bf16), 0, 1) * healthy(marks).astype(bf16)


def grad_kernel(place, eigen_0, eigen_1, act_0, act_1, give, keep, up, down, first_1, second_3, own, total):
    chunk, cut = give.shape[1], give.shape[2]
    total[...] = dot(eigen_0[...], act_0[...]) + dot(eigen_1[...], act_1[...])
    outs = ((own, 0, own, 1), (first_1, None, up, 1), (up, 0, down, 0), (down, 1, second_3, None))
    for s in range(4):
        base = (place[0] + s) % 4 * 2 * chunk
        mine = pl.ds(pl.multiple_of(base + place[1] * chunk, 16), chunk)
        other = pl.ds(pl.multiple_of(base + (1 - place[1]) * chunk, 16), chunk)
        give[s] = total[other, :cut].astype(bf16)
        keep[s] = total[mine, :cut].astype(bf16)
        for half in range(2):
            out, at = outs[s][2 * half : 2 * half + 2]
            value = total[pl.ds(pl.multiple_of(base + half * chunk, 16), chunk), cut:].astype(bf16)
            if at is None:
                out[...] = value
            else:
                out[at] = value


def second_kernel(keep, got_a, got_up, got_down, first_1, second_3, up, down, a_first_1, a_second_3, own_a):
    part = own_a.shape[1]
    rest = first_1.shape[1]
    up[:, :rest] = added(first_1[...], got_up[0]).astype(bf16)
    down[:, :rest] = added(second_3[...], got_down[0]).astype(bf16)

    def a_sum(s, half):
        rows = slice(half * part, (half + 1) * part)
        return added(keep[s, rows], got_a[s, rows]).astype(bf16)

    up[:part, rest:] = a_sum(2, 0)
    up[part:, rest:] = a_sum(1, 1)
    down[:part, rest:] = a_sum(2, 1)
    down[part:, rest:] = a_sum(3, 0)
    a_first_1[...] = a_sum(1, 0)
    a_second_3[...] = a_sum(3, 1)
    own_a[0] = a_sum(0, 0)
    own_a[1] = a_sum(0, 1)


def third_kernel(
    place, got_up, got_down, up, down, own_b, a_first_1, a_second_3, own_a, a_up, a_down, give, keep_b, keep_a
):
    part = own_a.shape[1]
    rest = own_b.shape[2]
    a_up[...] = added(a_first_1[...], up[:part, rest:]).astype(bf16)
    a_down[...] = added(a_second_3[...], down[:part, rest:]).astype(bf16)
    first = added(own_b[0], got_down[0], up[:, :rest])
    second = added(own_b[1], got_up[0], down[:, :rest])
    left = place[1] == 0
    give[...] = jnp.where(left, second, first).astype(bf16)
    keep_b[...] = jnp.where(left, first, second)
    keep_a[0] = added(own_a[0], down[part:, rest:])
    keep_a[1] = added(own_a[1], up[part:, rest:])


def cov_kernel(
    place, cot_0, cot_1, marks_0, marks_1, act_0, act_1, cols_0, cols_1, up, down, rest, turned, mine, cov_out, cov_in
):
    places = ((rest, 0, rest, 1), (rest, 2, up, 1), (up, 0, down, 0), (down, 1, rest, 3))
    tokens = cot_0.shape[0]
    rows = mine.shape[0] // 8
    mask_0, mask_1 = healthy(marks_0).astype(bf16), healthy(marks_1).astype(bf16)
    turned[:, :tokens] = jnp.swapaxes(cot_0[...], 0, 1) * mask_0
    turned[:, tokens:] = jnp.swapaxes(cot_1[...], 0, 1) * mask_1
    for s in range(4):
        for x in range(2):
            base = ((place[0] + s) % 4 * 4 + 2 * x + place[2]) * rows
            at = (2 * s + x) * rows
            mine[at : at + rows] = turned[pl.ds(pl.multiple_of(base, 16), rows), :]
    cov_out[...] = dot(mine[:, :tokens], cot_0[...]) + dot(mine[:, tokens:], cot_1[...])
    odd = place[3] % 2
    side = 0.0
    for cols, mask, act in ((cols_0, mask_0, act_0), (cols_1, mask_1, act_1)):
        own = jnp.where(odd == 0, cols[:, : 2 * rows].astype(f32), cols[:, 2 * rows :].astype(f32)).astype(bf16)
        side += dot(jnp.swapaxes(own, 0, 1) * mask, act[...])
    cov_in[...] = jnp.swapaxes(side, 0, 1)
    for s in range(4):
        for x in range(2):
            base = ((place[0] + s) % 4 * 4 + 2 * x) * rows
            pair = [cov_in[pl.ds(pl.multiple_of(base + k * rows, 16), rows), :] for k in range(2)]
            at = (2 * s + x) * rows
            out, index = places[s][2 * x : 2 * x + 2]
            out[index] = jnp.concatenate([cov_out[at : at + rows], *pair], 1).astype(bf16)


def squares_in_kernel(place, act_0, act_1, marks_0, marks_1, basis, out_in):
    total = 0.0
    for act, marks in ((act_0, marks_0), (act_1, marks_1)):
        tokens, columns = act.shape[0], basis.shape[1]
        lanes = min(128, columns)
        square = jnp.square(dot(act[...], basis[...]).astype(bf16).astype(f32))
        mask = jnp.swapaxes(jnp.broadcast_to(healthy(marks), (lanes, tokens)), 0, 1)
        total += jnp.sum(square * jnp.concatenate([mask] * (columns // lanes), 1), axis=0, keepdims=True)
    out_in[...] = total


def squares_out_kernel(place, marks_0, marks_1, eigen_0, eigen_1, out_out):
    width, tokens = eigen_0.shape
    lanes = min(128, tokens)
    count = jnp.sum(2.0 - healthy(marks_0) - healthy(marks_1), axis=1, keepdims=True)
    out_out[4:5, :] = jnp.broadcast_to(count, (1, width // 4))
    for at in range(0, width, width // 4):
        rows = slice(at, at + width // 4)
        square = jnp.square(eigen_0[rows].astype(f32)) + jnp.square(eigen_1[rows].astype(f32))
        square = sum(square[:, i : i + lanes] for i in range(0, tokens, lanes))
        out_out[at // (width // 4) : at // (width // 4) + 1, :] = jnp.sum(jnp.swapaxes(square, 0, 1), axis=0, keepdims=True)


def rows_kernel(place, own, got, out):
    for s in range(4):
        out[(place[0] + s) % 4, place[1]] = own[s]
        out[(place[0] + s) % 4, 1 - place[1]] = got[s]


def turn_kernel(
    place, keep_a, via_up, via_down, keep_b, got_b, basis, small, scale_in, scale_out, out, grad, total, lam_out, scales, rows_all
):
    y = pl.program_id(0)
    cut = keep_a.shape[2]
    part = keep_a.shape[1]
    chunk = 2 * part
    healthy_rows = rows_all - small[4:5, 0:1]

    @pl.when(y == 0)
    def _():
        grad[:part, :cut] = added(keep_a[0], via_up[...]).astype(bf16)
        grad[part:, :cut] = added(keep_a[1], via_down[...]).astype(bf16)
        grad[:, cut:] = added(keep_b[...], got_b[...]).astype(bf16)
        total[...] = jnp.zeros(total.shape, f32)
        wide = 2 * chunk
        scale = scale_out[:, pl.ds(pl.multiple_of(place[0] * wide, wide), wide)]
        lam = decay_rate * scale + blend_weight * small[pl.ds(place[0], 1), :] / healthy_rows
        lam = jnp.where(place[1] == 0, lam[:, :chunk], lam[:, chunk:]) * healthy_rows
        row = scale_in[pl.ds(place[2], 1), :]
        for k in range(4):
            halves = [row[:, i : i + chunk] for i in (k * chunk, (4 + k) * chunk)]
            swapped = jnp.concatenate(halves[::-1], 1)
            scales[k : k + 1, :] = jnp.where(place[3] < 4, jnp.concatenate(halves, 1), swapped)
        lam_out[...] = jnp.swapaxes(jnp.broadcast_to(lam, (lam_out.shape[1], chunk)), 0, 1)

    lam_in = decay_rate * scales[pl.ds(y, 1), :] + blend_weight * small[pl.ds(5 + y, 1), :] / healthy_rows
    rotated = dot(grad[...], basis[0])
    scaled = (rotated / (lam_out[:, :1] * lam_in + damping * healthy_rows)).astype(bf16)
    total[...] += dot(basis[0], scaled, ((1,), (1,)))

    @pl.when(y == 3)
    def _():
        rows, main = out.shape[1] * 2 // 3, out.shape[2]
        for d in range(16):
            block = total[d * rows : (d + 1) * rows, :]
            out[d, :rows, :] = block[:, :main].astype(bf16)
            side = block[:, main:]
            out[d, rows:, :] = jnp.concatenate([side[: rows // 2], side[rows // 2 :]], 1).astype(bf16)


def last_kernel(spread, basis_out, out, total):
    z = pl.program_id(0)
    rows, main = out.shape[1], spread.shape[2]

    def block(at):
        side = spread[at, rows:, :]
        side = jnp.concatenate([side[:, : main // 2], side[:, main // 2 :]], 0)
        return jnp.concatenate([spread[at, :rows, :], side], 1)

    lhs = [jnp.concatenate([block(4 * z + a), block(4 * z + 2 + a)], 1) for a in range(2)]
    part = dot(jnp.concatenate(lhs, 0), basis_out[...], ((1,), (1,)))

    @pl.when(z == 0)
    def _():
        total[...] = part

    @pl.when(z > 0)
    def _():
        total[...] += part

    @pl.when(z == 3)
    def _():
        out[0] = total[:rows].astype(bf16)
        out[1] = total[rows:].astype(bf16)


def per_device(
    activations,
    cotangents,
    basis_in,
    basis_out,
    factor_in,
    factor_out,
    scale_in,
    scale_out,
    overflow,
):
    tokens = activations.shape[0]
    width = scale_in.shape[1]
    rows = factor_in.shape[0]
    cols = factor_in.shape[2]
    chunk = width // 8
    wide = width // 4
    cut = width // 3
    dp = lax.axis_index("dp")
    fac = lax.axis_index("factor")
    core, x, z = dp % 2, (dp // 2) % 2, dp // 4
    place = jnp.stack([z, x, core, fac]).astype(jnp.int32)

    basis_keep = lax.dynamic_index_in_dim(basis_in, core, 1, keepdims=False)
    basis_give = lax.dynamic_index_in_dim(basis_in, 1 - core, 1, keepdims=False)
    basis_got = lax.ppermute(basis_give, "dp", CORE)
    marks = overflow.reshape(1, tokens)
    marks_got = lax.ppermute(marks, "dp", CORE)
    cot_got = lax.ppermute(cotangents, "dp", CORE)
    act_give = lax.dynamic_slice_in_dim(activations, (1 - core) * width, width, 1)
    act_got = lax.ppermute(act_give, "dp", CORE)

    def rotate(place, at, before):
        return pl.pallas_call(
            rotate_kernel,
            out_shape=shape_of(width, tokens),
            grid_spec=pltpu.PrefetchScalarGridSpec(
                num_scalar_prefetch=1,
                grid=(2,),
                in_specs=[
                    whole((tokens, width)),
                    whole((1, tokens)),
                    pl.BlockSpec((width, wide), lambda i, p: (0, at + i)),
                ]
                + [pl.BlockSpec(memory_space=pl.ANY)] * len(before),
                out_specs=pl.BlockSpec((wide, tokens), lambda i, p: (at + i, 0)),
            ),
            input_output_aliases={4: 0} if before else {},
            compiler_params=EARLY,
            name="rotate_kernel",
        )(place, cotangents, marks, basis_out, *before)

    eigen_half = rotate(after(place, act_give, basis_give), 0, ())
    basis_mine = after(basis_keep, eigen_half)
    basis_chip = jnp.where(
        core == 0,
        jnp.concatenate([basis_mine, basis_got], 0),
        jnp.concatenate([basis_got, basis_mine], 0),
    )
    basis_x_hi = lax.ppermute(basis_chip, "factor", XHI)
    eigen = rotate(after(place, basis_chip, marks_got), 2, (eigen_half,))
    eigen_got = lax.ppermute(after(eigen, basis_x_hi), "dp", CORE)
    basis_pair = jnp.concatenate([after(basis_chip, eigen), basis_x_hi], 1)
    basis_z = [lax.ppermute(basis_pair, "dp", to_z(4 - s)) for s in (1, 2, 3)]

    def own_block(n, at):
        return pl.BlockSpec((tokens, n), lambda i, p: (0, at(i, p)))

    columns = width + 2 * cols
    cov_up, cov_down, cov_rest = placed(
        cov_kernel,
        after(place, basis_pair),
        (1,),
        [whole((tokens, width))] * 2
        + [whole((1, tokens))] * 2
        + [own_block(width, lambda i, p: p[2]), whole((tokens, width))]
        + [own_block(wide, lambda i, p: p[2] * 4 + p[3] // 2), own_block(wide, lambda i, p: p[3] // 2)],
        [shape_of(n, rows, columns) for n in (2, 2, 4)],
        (cotangents, cot_got, marks, marks_got, activations, act_got, activations, act_got),
        scratch=[
            pltpu.VMEM((width, 2 * tokens), bf16),
            pltpu.VMEM((8 * rows, 2 * tokens), bf16),
            pltpu.VMEM((8 * rows, width), f32),
            pltpu.VMEM((width, cols), f32),
        ],
        params=EARLY,
    )
    cov_got_up, cov_got_down = send_z(cov_up, cov_down)

    basis_four = jnp.stack([after(basis_pair, cov_up), *basis_z])
    basis_x_lo = lax.ppermute(basis_four, "dp", XLO)

    single = shape_of(chunk, width - cut)
    pair = shape_of(2, chunk, width - cut)
    four = shape_of(4, chunk, cut)
    give, keep, up, down, first_1, second_3, own_b = placed(
        grad_kernel,
        after(place, basis_four),
        (1,),
        [whole((width, tokens))] * 2
        + [pl.BlockSpec((tokens, width), lambda i, p: (0, p[2])), whole((tokens, width))],
        [four, four, pair, pair, single, single, pair],
        (eigen, eigen_got, activations, act_got),
        scratch=[pltpu.VMEM((width, width), f32)],
    )
    scale_row = after(scale_out, own_b).reshape(1, width)
    (squares_out,) = placed(
        squares_out_kernel,
        after(place, own_b),
        (1,),
        [whole((1, tokens))] * 2 + [whole((width, tokens))] * 2,
        [shape_of(5, wide, dtype=f32)],
        (marks, marks_got, eigen, eigen_got),
    )
    (basis_rows,) = placed(
        rows_kernel,
        after(place, own_b, cov_got_up, cov_got_down, scale_row, squares_out),
        (1,),
        [whole(basis_four.shape)] * 2,
        [shape_of(4, 2, 2 * rows, 2 * cols)],
        (basis_four, basis_x_lo),
    )
    basis_rows = basis_rows.reshape(width, 2 * cols)
    basis_all = lax.all_gather(basis_rows, "factor", axis=0, axis_index_groups=SAME_XHI)
    (squares_in,) = placed(
        squares_in_kernel,
        place,
        (1,),
        [pl.BlockSpec((tokens, width), lambda i, p: (0, p[2])), whole((tokens, width))]
        + [whole((1, tokens))] * 2
        + [whole((width, 2 * cols))],
        [shape_of(1, 2 * cols, dtype=f32)],
        (activations, act_got, marks, marks_got, basis_rows),
    )
    y = fac % 4

    def pair_y(own, got, first):
        return jnp.where(first, jnp.concatenate([own, got], 0), jnp.concatenate([got, own], 0))

    by_y = pair_y(squares_in, lax.ppermute(squares_in, "factor", swap_y(1)), y % 2 == 0)
    by_y = pair_y(by_y, lax.ppermute(by_y, "factor", swap_y(2)), y < 2)
    give, up, down = lax.optimization_barrier((give, up, down, basis_x_lo))[:3]
    got_a = lax.ppermute(give, "dp", XLO)
    got_up, got_down = send_z(up, down)
    part = chunk // 2
    second_up, second_down, a_first_1, a_second_3, own_a = pl.pallas_call(
        second_kernel,
        out_shape=(
            shape_of(chunk, width),
            shape_of(chunk, width),
            shape_of(part, cut),
            shape_of(part, cut),
            shape_of(2, part, cut),
        ),
        compiler_params=PARAMS,
        name="second_kernel",
    )(after(keep, by_y), got_a, got_up, got_down, first_1, second_3)
    second_got_up, second_got_down = send_z(second_up, second_down)

    small = jnp.concatenate([squares_out, after(by_y, second_up, second_down)], 0)
    small = small + lax.ppermute(small, "dp", XLO)
    small = added(small, *[lax.ppermute(small, "dp", to_z(i)) for i in (1, 3, 2)])
    cov_late = after(cov_rest, small)
    cov_next = forward_z(cov_got_up, cov_got_down, cov_late[2], cov_late[3])
    near = pl.BlockSpec((1, chunk, width - cut), lambda i, p: (1, 0, 0))
    third_in = (second_got_up, second_got_down, own_b, a_first_1, a_second_3, own_a)
    third_up, third_down, b_give, b_keep, a_keep = placed(
        third_kernel,
        after(place, small),
        (1,),
        [near, near] + [whole(t.shape) for t in third_in],
        [
            shape_of(part, cut),
            shape_of(part, cut),
            shape_of(chunk, width - cut),
            shape_of(chunk, width - cut, dtype=f32),
            shape_of(2, part, cut, dtype=f32),
        ],
        (got_up, got_down, *third_in),
    )
    b_got = lax.ppermute(b_give, "dp", XLO)
    a_via_up, a_via_down = send_z(third_up, third_down)

    healthy_rows = f32(tokens * lax.axis_size("dp")) - small[4, 0]

    cov_next = lax.optimization_barrier((*cov_next, b_got, a_via_up, a_via_down, healthy_rows))[:2]
    cov_via_up, cov_via_down = send_z(*cov_next)

    turn_in = (a_keep, a_via_up, a_via_down, b_keep, b_got)
    (turned,) = placed(
        functools.partial(turn_kernel, rows_all=float(tokens * lax.axis_size("dp"))),
        place,
        (4,),
        [whole(t.shape) for t in turn_in]
        + [pl.BlockSpec((1, width, 2 * cols), lambda i, p: (i, 0, 0))]
        + [whole((9, wide)), whole((2, width)), whole((1, width))],
        [shape_of(16, rows * 3 // 2, chunk * 2 // 3)],
        (*turn_in, basis_all, small, scale_in, scale_row),
        scratch=[
            pltpu.VMEM((chunk, width), bf16),
            pltpu.VMEM((width, chunk), f32),
            pltpu.VMEM((chunk, 128), f32),
            pltpu.VMEM((4, wide), f32),
        ],
        name="turn_kernel",
    )
    cov_rest = after(cov_rest, turned)
    cov_first = added(cov_rest[0], cov_got_down[1], cov_via_up)
    cov_second = added(cov_rest[1], cov_got_up[1], cov_via_down)
    cov_give = jnp.where(x == 0, cov_second, cov_first).astype(bf16)
    cov_keep = jnp.where(x == 0, cov_first, cov_second)
    cov_sum = added(cov_keep, lax.ppermute(cov_give, "dp", XLO))
    sum_out = cov_sum[:, :width]
    sum_in = cov_sum[:, width:].reshape(rows, 2, cols)
    in_keep = lax.dynamic_index_in_dim(sum_in, core, 1, keepdims=False)
    in_give = lax.dynamic_index_in_dim(sum_in, 1 - core, 1, keepdims=False).astype(bf16)
    in_got = lax.ppermute(in_give, "dp", CORE).astype(f32)

    spread = lax.all_to_all(turned, "dp", split_axis=0, concat_axis=0)
    result = pl.pallas_call(
        last_kernel,
        out_shape=shape_of(2, rows, width),
        grid=(4,),
        in_specs=[whole(spread.shape), pl.BlockSpec((width, wide), lambda i: (0, i))],
        out_specs=whole((2, rows, width)),
        scratch_shapes=[pltpu.VMEM((2 * rows, width), f32)],
        compiler_params=PARAMS,
        name="last_kernel",
    )(spread, basis_out)

    sum_in = jnp.where(core == 0, jnp.stack([in_keep, in_got], 1), jnp.stack([in_got, in_keep], 1))
    new_factor_in = decay_rate * factor_in + blend_weight * sum_in / healthy_rows
    new_factor_out = decay_rate * factor_out + blend_weight * sum_out / healthy_rows
    return (jnp.swapaxes(result, 0, 1), new_factor_in, new_factor_out)


def solution(mesh):
    in_specs = (
        P("dp", None),
        P("dp", "factor"),
        P("dp", None, "factor"),
        P("factor", None),
        P("dp", None, "factor"),
        P("dp", "factor"),
        P(),
        P("factor"),
        P("dp"),
    )
    out_specs = (P("dp", None, "factor"), P("dp", None, "factor"), P("dp", "factor"))
    return jax.shard_map(
        per_device, mesh=mesh, in_specs=in_specs, out_specs=out_specs, check_vma=False
    )
```

```python
import functools

import jax
import jax.numpy as jnp
from jax import lax
from jax.experimental import pallas as pl
from jax.experimental.pallas import tpu as pltpu
from jax.sharding import PartitionSpec as P

decay_rate = 0.9
damping = 0.001
blend_weight = 1.0 - decay_rate

f32 = jnp.float32
bf16 = jnp.bfloat16

CORE = [(i, i ^ 1) for i in range(16)]
XLO = [(i, i ^ 2) for i in range(16)]
XHI = [(j, j ^ 4) for j in range(8)]
SAME_XHI = [[0, 1, 2, 3], [4, 5, 6, 7]]
PARAMS = pltpu.CompilerParams(vmem_limit_bytes=64 * 2**20)
EARLY = pltpu.CompilerParams(vmem_limit_bytes=56 * 2**20)


def to_z(s):
    return [(i, ((i >> 2) + s) % 4 * 4 + (i & 3)) for i in range(16)]


def swap_z(bits):
    return [(i, i ^ (bits * 4)) for i in range(16)]


def swap_y(bits):
    return [(j, j ^ bits) for j in range(8)]


UP, DOWN = to_z(1), to_z(3)


def dot(a, b, contract=((1,), (0,)), **kwargs):
    return lax.dot_general(a, b, (contract, ((), ())), preferred_element_type=f32, **kwargs)


def added(*parts):
    total = parts[0].astype(f32)
    for part in parts[1:]:
        total = total + part.astype(f32)
    return total


def after(value, *others):
    return lax.optimization_barrier((value, *others))[0]


def send_z(up, down):
    return lax.ppermute(up, "dp", UP), lax.ppermute(down, "dp", DOWN)


def forward_z(got_up, got_down, first_1, second_3):
    return added(first_1, got_up[0]).astype(bf16), added(second_3, got_down[0]).astype(bf16)


def shape_of(*dims, dtype=bf16):
    return jax.ShapeDtypeStruct(dims, dtype)


def whole(shape):
    return pl.BlockSpec(shape, lambda *_: (0,) * len(shape))


def placed(kernel, place, grid, in_specs, out_shapes, operands, out_specs=None, scratch=(), name=None, params=PARAMS):
    return pl.pallas_call(
        kernel,
        out_shape=out_shapes,
        grid_spec=pltpu.PrefetchScalarGridSpec(
            num_scalar_prefetch=1,
            grid=grid,
            in_specs=in_specs,
            out_specs=out_specs or [whole(s.shape) for s in out_shapes],
            scratch_shapes=list(scratch),
        ),
        compiler_params=params,
        name=name or kernel.__name__,
    )(place, *operands)


def healthy(marks):
    return (marks[...] == 0).astype(f32)


def rotate_kernel(place, cot, marks, basis, *refs):
    refs[-1][...] = jnp.swapaxes(dot(cot[...], basis[...]).astype(bf16), 0, 1) * healthy(marks).astype(bf16)


def grad_kernel(place, eigen_0, eigen_1, act_0, act_1, give, keep, up, down, first_1, second_3, own, total):
    chunk, cut = give.shape[1], give.shape[2]
    total[...] = dot(eigen_0[...], act_0[...]) + dot(eigen_1[...], act_1[...])
    outs = ((own, 0, own, 1), (first_1, None, up, 1), (up, 0, down, 0), (down, 1, second_3, None))
    for s in range(4):
        base = (place[0] + s) % 4 * 2 * chunk
        mine = pl.ds(pl.multiple_of(base + place[1] * chunk, 16), chunk)
        other = pl.ds(pl.multiple_of(base + (1 - place[1]) * chunk, 16), chunk)
        give[s] = total[other, :cut].astype(bf16)
        keep[s] = total[mine, :cut].astype(bf16)
        for half in range(2):
            out, at = outs[s][2 * half : 2 * half + 2]
            value = total[pl.ds(pl.multiple_of(base + half * chunk, 16), chunk), cut:].astype(bf16)
            if at is None:
                out[...] = value
            else:
                out[at] = value


def second_kernel(keep, got_a, got_up, got_down, first_1, second_3, up, down, a_first_1, a_second_3, own_a):
    part = own_a.shape[1]
    rest = first_1.shape[1]
    up[:, :rest] = added(first_1[...], got_up[0]).astype(bf16)
    down[:, :rest] = added(second_3[...], got_down[0]).astype(bf16)

    def a_sum(s, half):
        rows = slice(half * part, (half + 1) * part)
        return added(keep[s, rows], got_a[s, rows]).astype(bf16)

    up[:part, rest:] = a_sum(2, 0)
    up[part:, rest:] = a_sum(1, 1)
    down[:part, rest:] = a_sum(2, 1)
    down[part:, rest:] = a_sum(3, 0)
    a_first_1[...] = a_sum(1, 0)
    a_second_3[...] = a_sum(3, 1)
    own_a[0] = a_sum(0, 0)
    own_a[1] = a_sum(0, 1)


def third_kernel(
    place, got_up, got_down, up, down, own_b, a_first_1, a_second_3, own_a, a_up, a_down, give, keep_b, keep_a
):
    part = own_a.shape[1]
    rest = own_b.shape[2]
    a_up[...] = added(a_first_1[...], up[:part, rest:]).astype(bf16)
    a_down[...] = added(a_second_3[...], down[:part, rest:]).astype(bf16)
    first = added(own_b[0], got_down[0], up[:, :rest])
    second = added(own_b[1], got_up[0], down[:, :rest])
    left = place[1] == 0
    give[...] = jnp.where(left, second, first).astype(bf16)
    keep_b[...] = jnp.where(left, first, second)
    keep_a[0] = added(own_a[0], down[part:, rest:])
    keep_a[1] = added(own_a[1], up[part:, rest:])


def cov_kernel(
    place, cot_0, cot_1, marks_0, marks_1, act_0, act_1, cols_0, cols_1, up, down, rest, turned, mine, cov_out, cov_in
):
    places = ((rest, 0, rest, 1), (rest, 2, up, 1), (up, 0, down, 0), (down, 1, rest, 3))
    tokens = cot_0.shape[0]
    rows = mine.shape[0] // 8
    mask_0, mask_1 = healthy(marks_0).astype(bf16), healthy(marks_1).astype(bf16)
    turned[:, :tokens] = jnp.swapaxes(cot_0[...], 0, 1) * mask_0
    turned[:, tokens:] = jnp.swapaxes(cot_1[...], 0, 1) * mask_1
    for s in range(4):
        for x in range(2):
            base = ((place[0] + s) % 4 * 4 + 2 * x + place[2]) * rows
            at = (2 * s + x) * rows
            mine[at : at + rows] = turned[pl.ds(pl.multiple_of(base, 16), rows), :]
    cov_out[...] = dot(mine[:, :tokens], cot_0[...]) + dot(mine[:, tokens:], cot_1[...])
    odd = place[3] % 2
    side = 0.0
    for cols, mask, act in ((cols_0, mask_0, act_0), (cols_1, mask_1, act_1)):
        own = jnp.where(odd == 0, cols[:, : 2 * rows].astype(f32), cols[:, 2 * rows :].astype(f32)).astype(bf16)
        side += dot(jnp.swapaxes(own, 0, 1) * mask, act[...])
    cov_in[...] = jnp.swapaxes(side, 0, 1)
    for s in range(4):
        for x in range(2):
            base = ((place[0] + s) % 4 * 4 + 2 * x) * rows
            pair = [cov_in[pl.ds(pl.multiple_of(base + k * rows, 16), rows), :] for k in range(2)]
            at = (2 * s + x) * rows
            out, index = places[s][2 * x : 2 * x + 2]
            out[index] = jnp.concatenate([cov_out[at : at + rows], *pair], 1).astype(bf16)


def squares_in_kernel(place, act_0, act_1, marks_0, marks_1, basis, out_in):
    total = 0.0
    for act, marks in ((act_0, marks_0), (act_1, marks_1)):
        tokens, columns = act.shape[0], basis.shape[1]
        lanes = min(128, columns)
        square = jnp.square(dot(act[...], basis[...]).astype(bf16).astype(f32))
        mask = jnp.swapaxes(jnp.broadcast_to(healthy(marks), (lanes, tokens)), 0, 1)
        total += jnp.sum(square * jnp.concatenate([mask] * (columns // lanes), 1), axis=0, keepdims=True)
    out_in[...] = total


def squares_out_kernel(place, marks_0, marks_1, eigen_0, eigen_1, out_out):
    width, tokens = eigen_0.shape
    lanes = min(128, tokens)
    count = jnp.sum(2.0 - healthy(marks_0) - healthy(marks_1), axis=1, keepdims=True)
    out_out[4:5, :] = jnp.broadcast_to(count, (1, width // 4))
    for at in range(0, width, width // 4):
        rows = slice(at, at + width // 4)
        square = jnp.square(eigen_0[rows].astype(f32)) + jnp.square(eigen_1[rows].astype(f32))
        square = sum(square[:, i : i + lanes] for i in range(0, tokens, lanes))
        out_out[at // (width // 4) : at // (width // 4) + 1, :] = jnp.sum(jnp.swapaxes(square, 0, 1), axis=0, keepdims=True)


def rows_kernel(place, own, got, out):
    for s in range(4):
        out[(place[0] + s) % 4, place[1]] = own[s]
        out[(place[0] + s) % 4, 1 - place[1]] = got[s]


def turn_kernel(
    place, keep_a, via_up, via_down, keep_b, got_b, basis, small, scale_in, scale_out, out, grad, total, lam_out, scales, rows_all
):
    y = pl.program_id(0)
    cut = keep_a.shape[2]
    part = keep_a.shape[1]
    chunk = 2 * part
    healthy_rows = rows_all - small[4:5, 0:1]

    @pl.when(y == 0)
    def _():
        grad[:part, :cut] = added(keep_a[0], via_up[...]).astype(bf16)
        grad[part:, :cut] = added(keep_a[1], via_down[...]).astype(bf16)
        grad[:, cut:] = added(keep_b[...], got_b[...]).astype(bf16)
        total[...] = jnp.zeros(total.shape, f32)
        wide = 2 * chunk
        scale = scale_out[:, pl.ds(pl.multiple_of(place[0] * wide, wide), wide)]
        lam = decay_rate * scale + blend_weight * small[pl.ds(place[0], 1), :] / healthy_rows
        lam = jnp.where(place[1] == 0, lam[:, :chunk], lam[:, chunk:]) * healthy_rows
        row = scale_in[pl.ds(place[2], 1), :]
        for k in range(4):
            halves = [row[:, i : i + chunk] for i in (k * chunk, (4 + k) * chunk)]
            swapped = jnp.concatenate(halves[::-1], 1)
            scales[k : k + 1, :] = jnp.where(place[3] < 4, jnp.concatenate(halves, 1), swapped)
        lam_out[...] = jnp.swapaxes(jnp.broadcast_to(lam, (lam_out.shape[1], chunk)), 0, 1)

    lam_in = decay_rate * scales[pl.ds(y, 1), :] + blend_weight * small[pl.ds(5 + y, 1), :] / healthy_rows
    rotated = dot(grad[...], basis[0])
    scaled = (rotated / (lam_out[:, :1] * lam_in + damping * healthy_rows)).astype(bf16)
    total[...] += dot(basis[0], scaled, ((1,), (1,)))

    @pl.when(y == 3)
    def _():
        rows, main = out.shape[1] * 2 // 3, out.shape[2]
        for d in range(16):
            block = total[d * rows : (d + 1) * rows, :]
            out[d, :rows, :] = block[:, :main].astype(bf16)
            side = block[:, main:]
            out[d, rows:, :] = jnp.concatenate([side[: rows // 2], side[rows // 2 :]], 1).astype(bf16)


def last_kernel(spread, basis_out, out, total):
    z = pl.program_id(0)
    rows, main = out.shape[1], spread.shape[2]

    def block(at):
        side = spread[at, rows:, :]
        side = jnp.concatenate([side[:, : main // 2], side[:, main // 2 :]], 0)
        return jnp.concatenate([spread[at, :rows, :], side], 1)

    lhs = [jnp.concatenate([block(4 * z + a), block(4 * z + 2 + a)], 1) for a in range(2)]
    part = dot(jnp.concatenate(lhs, 0), basis_out[...], ((1,), (1,)))

    @pl.when(z == 0)
    def _():
        total[...] = part

    @pl.when(z > 0)
    def _():
        total[...] += part

    @pl.when(z == 3)
    def _():
        out[0] = total[:rows].astype(bf16)
        out[1] = total[rows:].astype(bf16)


def per_device(
    activations,
    cotangents,
    basis_in,
    basis_out,
    factor_in,
    factor_out,
    scale_in,
    scale_out,
    overflow,
):
    tokens = activations.shape[0]
    width = scale_in.shape[1]
    rows = factor_in.shape[0]
    cols = factor_in.shape[2]
    chunk = width // 8
    wide = width // 4
    cut = width // 3
    dp = lax.axis_index("dp")
    fac = lax.axis_index("factor")
    core, x, z = dp % 2, (dp // 2) % 2, dp // 4
    place = jnp.stack([z, x, core, fac]).astype(jnp.int32)

    basis_keep = lax.dynamic_index_in_dim(basis_in, core, 1, keepdims=False)
    basis_give = lax.dynamic_index_in_dim(basis_in, 1 - core, 1, keepdims=False)
    basis_got = lax.ppermute(basis_give, "dp", CORE)
    marks = overflow.reshape(1, tokens)
    marks_got = lax.ppermute(marks, "dp", CORE)
    cot_got = lax.ppermute(cotangents, "dp", CORE)
    act_give = lax.dynamic_slice_in_dim(activations, (1 - core) * width, width, 1)
    act_got = lax.ppermute(act_give, "dp", CORE)

    def rotate(place, at, before):
        return pl.pallas_call(
            rotate_kernel,
            out_shape=shape_of(width, tokens),
            grid_spec=pltpu.PrefetchScalarGridSpec(
                num_scalar_prefetch=1,
                grid=(2,),
                in_specs=[
                    whole((tokens, width)),
                    whole((1, tokens)),
                    pl.BlockSpec((width, wide), lambda i, p: (0, at + i)),
                ]
                + [pl.BlockSpec(memory_space=pl.ANY)] * len(before),
                out_specs=pl.BlockSpec((wide, tokens), lambda i, p: (at + i, 0)),
            ),
            input_output_aliases={4: 0} if before else {},
            compiler_params=EARLY,
            name="rotate_kernel",
        )(place, cotangents, marks, basis_out, *before)

    eigen_half = rotate(after(place, act_give, basis_give), 0, ())
    basis_mine = after(basis_keep, eigen_half)
    basis_chip = jnp.where(
        core == 0,
        jnp.concatenate([basis_mine, basis_got], 0),
        jnp.concatenate([basis_got, basis_mine], 0),
    )
    basis_x_hi = lax.ppermute(basis_chip, "factor", XHI)
    eigen = rotate(after(place, basis_chip, marks_got), 2, (eigen_half,))
    eigen_got = lax.ppermute(after(eigen, basis_x_hi), "dp", CORE)
    basis_pair = jnp.concatenate([after(basis_chip, eigen), basis_x_hi], 1)
    basis_z = [lax.ppermute(basis_pair, "dp", to_z(4 - s)) for s in (1, 2, 3)]

    def own_block(n, at):
        return pl.BlockSpec((tokens, n), lambda i, p: (0, at(i, p)))

    columns = width + 2 * cols
    cov_up, cov_down, cov_rest = placed(
        cov_kernel,
        after(place, basis_pair),
        (1,),
        [whole((tokens, width))] * 2
        + [whole((1, tokens))] * 2
        + [own_block(width, lambda i, p: p[2]), whole((tokens, width))]
        + [own_block(wide, lambda i, p: p[2] * 4 + p[3] // 2), own_block(wide, lambda i, p: p[3] // 2)],
        [shape_of(n, rows, columns) for n in (2, 2, 4)],
        (cotangents, cot_got, marks, marks_got, activations, act_got, activations, act_got),
        scratch=[
            pltpu.VMEM((width, 2 * tokens), bf16),
            pltpu.VMEM((8 * rows, 2 * tokens), bf16),
            pltpu.VMEM((8 * rows, width), f32),
            pltpu.VMEM((width, cols), f32),
        ],
        params=EARLY,
    )
    cov_got_up, cov_got_down = send_z(cov_up, cov_down)

    basis_four = jnp.stack([after(basis_pair, cov_up), *basis_z])
    basis_x_lo = lax.ppermute(basis_four, "dp", XLO)

    single = shape_of(chunk, width - cut)
    pair = shape_of(2, chunk, width - cut)
    four = shape_of(4, chunk, cut)
    give, keep, up, down, first_1, second_3, own_b = placed(
        grad_kernel,
        after(place, basis_four),
        (1,),
        [whole((width, tokens))] * 2
        + [pl.BlockSpec((tokens, width), lambda i, p: (0, p[2])), whole((tokens, width))],
        [four, four, pair, pair, single, single, pair],
        (eigen, eigen_got, activations, act_got),
        scratch=[pltpu.VMEM((width, width), f32)],
    )
    scale_row = after(scale_out, own_b).reshape(1, width)
    (squares_out,) = placed(
        squares_out_kernel,
        after(place, own_b),
        (1,),
        [whole((1, tokens))] * 2 + [whole((width, tokens))] * 2,
        [shape_of(5, wide, dtype=f32)],
        (marks, marks_got, eigen, eigen_got),
    )
    (basis_rows,) = placed(
        rows_kernel,
        after(place, own_b, cov_got_up, cov_got_down, scale_row, squares_out),
        (1,),
        [whole(basis_four.shape)] * 2,
        [shape_of(4, 2, 2 * rows, 2 * cols)],
        (basis_four, basis_x_lo),
    )
    basis_rows = basis_rows.reshape(width, 2 * cols)
    basis_all = lax.all_gather(basis_rows, "factor", axis=0, axis_index_groups=SAME_XHI)
    (squares_in,) = placed(
        squares_in_kernel,
        place,
        (1,),
        [pl.BlockSpec((tokens, width), lambda i, p: (0, p[2])), whole((tokens, width))]
        + [whole((1, tokens))] * 2
        + [whole((width, 2 * cols))],
        [shape_of(1, 2 * cols, dtype=f32)],
        (activations, act_got, marks, marks_got, basis_rows),
    )
    y = fac % 4

    def pair_y(own, got, first):
        return jnp.where(first, jnp.concatenate([own, got], 0), jnp.concatenate([got, own], 0))

    by_y = pair_y(squares_in, lax.ppermute(squares_in, "factor", swap_y(1)), y % 2 == 0)
    by_y = pair_y(by_y, lax.ppermute(by_y, "factor", swap_y(2)), y < 2)
    give, up, down = lax.optimization_barrier((give, up, down, basis_x_lo))[:3]
    got_a = lax.ppermute(give, "dp", XLO)
    got_up, got_down = send_z(up, down)
    part = chunk // 2
    second_up, second_down, a_first_1, a_second_3, own_a = pl.pallas_call(
        second_kernel,
        out_shape=(
            shape_of(chunk, width),
            shape_of(chunk, width),
            shape_of(part, cut),
            shape_of(part, cut),
            shape_of(2, part, cut),
        ),
        compiler_params=PARAMS,
        name="second_kernel",
    )(after(keep, by_y), got_a, got_up, got_down, first_1, second_3)
    second_got_up, second_got_down = send_z(second_up, second_down)

    small = jnp.concatenate([squares_out, after(by_y, second_up, second_down)], 0)
    small = small + lax.ppermute(small, "dp", XLO)
    small = added(small, *[lax.ppermute(small, "dp", to_z(i)) for i in (1, 3, 2)])
    near = pl.BlockSpec((1, chunk, width - cut), lambda i, p: (1, 0, 0))
    third_in = (second_got_up, second_got_down, own_b, a_first_1, a_second_3, own_a)
    third_up, third_down, b_give, b_keep, a_keep = placed(
        third_kernel,
        after(place, small),
        (1,),
        [near, near] + [whole(t.shape) for t in third_in],
        [
            shape_of(part, cut),
            shape_of(part, cut),
            shape_of(chunk, width - cut),
            shape_of(chunk, width - cut, dtype=f32),
            shape_of(2, part, cut, dtype=f32),
        ],
        (got_up, got_down, *third_in),
    )
    healthy_rows = f32(tokens * lax.axis_size("dp")) - after(small, b_give)[4, 0]
    b_got = lax.ppermute(b_give, "dp", XLO)
    third_up, third_down = lax.optimization_barrier((third_up, third_down, healthy_rows))[:2]
    a_via_up, a_via_down = send_z(third_up, third_down)


    cov_next = forward_z(cov_got_up, cov_got_down, cov_rest[2], cov_rest[3])
    cov_next = lax.optimization_barrier((*cov_next, a_via_up, a_via_down, b_got, healthy_rows))[:2]
    cov_via_up, cov_via_down = send_z(*cov_next)

    turn_in = (a_keep, a_via_up, a_via_down, b_keep, b_got)
    (turned,) = placed(
        functools.partial(turn_kernel, rows_all=float(tokens * lax.axis_size("dp"))),
        place,
        (4,),
        [whole(t.shape) for t in turn_in]
        + [pl.BlockSpec((1, width, 2 * cols), lambda i, p: (i, 0, 0))]
        + [whole((9, wide)), whole((2, width)), whole((1, width))],
        [shape_of(16, rows * 3 // 2, chunk * 2 // 3)],
        (*turn_in, basis_all, small, scale_in, scale_row),
        scratch=[
            pltpu.VMEM((chunk, width), bf16),
            pltpu.VMEM((width, chunk), f32),
            pltpu.VMEM((chunk, 128), f32),
            pltpu.VMEM((4, wide), f32),
        ],
        name="turn_kernel",
    )
    cov_rest = after(cov_rest, turned)
    cov_first = added(cov_rest[0], cov_got_down[1], cov_via_up)
    cov_second = added(cov_rest[1], cov_got_up[1], cov_via_down)
    cov_give = jnp.where(x == 0, cov_second, cov_first).astype(bf16)
    cov_keep = jnp.where(x == 0, cov_first, cov_second)
    cov_sum = added(cov_keep, lax.ppermute(cov_give, "dp", XLO))
    sum_out = cov_sum[:, :width]
    sum_in = cov_sum[:, width:].reshape(rows, 2, cols)
    in_keep = lax.dynamic_index_in_dim(sum_in, core, 1, keepdims=False)
    in_give = lax.dynamic_index_in_dim(sum_in, 1 - core, 1, keepdims=False).astype(bf16)
    in_got = lax.ppermute(in_give, "dp", CORE).astype(f32)

    spread = lax.all_to_all(turned, "dp", split_axis=0, concat_axis=0)
    result = pl.pallas_call(
        last_kernel,
        out_shape=shape_of(2, rows, width),
        grid=(4,),
        in_specs=[whole(spread.shape), pl.BlockSpec((width, wide), lambda i: (0, i))],
        out_specs=whole((2, rows, width)),
        scratch_shapes=[pltpu.VMEM((2 * rows, width), f32)],
        compiler_params=PARAMS,
        name="last_kernel",
    )(spread, basis_out)

    sum_in = jnp.where(core == 0, jnp.stack([in_keep, in_got], 1), jnp.stack([in_got, in_keep], 1))
    new_factor_in = decay_rate * factor_in + blend_weight * sum_in / healthy_rows
    new_factor_out = decay_rate * factor_out + blend_weight * sum_out / healthy_rows
    return (jnp.swapaxes(result, 0, 1), new_factor_in, new_factor_out)


def solution(mesh):
    in_specs = (
        P("dp", None),
        P("dp", "factor"),
        P("dp", None, "factor"),
        P("factor", None),
        P("dp", None, "factor"),
        P("dp", "factor"),
        P(),
        P("factor"),
        P("dp"),
    )
    out_specs = (P("dp", None, "factor"), P("dp", None, "factor"), P("dp", "factor"))
    return jax.shard_map(
        per_device, mesh=mesh, in_specs=in_specs, out_specs=out_specs, check_vma=False
    )
```
